128 devices in a mesh: ctx: 16 (over y_lo, x, core), head: 8 (over z, y_hi).
Axes of the slice: x: 4, y: 4 (y_hi: 2, y_lo: 2; y = y_hi * 2 + y_lo), z: 4, core: 2. Of those that a mesh axis runs over, the one named last changes fastest.
Arguments:
- q_nope: bfloat16 [2048, 16384], P('ctx', 'head'), may hold values from -9 to 9
- q_rope: bfloat16 [2048, 8192], P('ctx', 'head'), may hold values from -200 to 200
- latent: bfloat16 [2048, 512], P('ctx'), may hold values from -350 to 350
- k_rope: bfloat16 [2048, 64], P('ctx'), may hold values from -3 to 3
- kv_gain: float32 [512], replicated, may hold values from 0.5 to 2
- w_uk: bfloat16 [512, 16384], P(None, 'head'), may hold values from -0.25 to 0.25
- w_uv: bfloat16 [512, 16384], P(None, 'head'), may hold values from -0.25 to 0.25
- w_out: bfloat16 [16384, 7168], P('head', 'ctx'), may hold values from -0.125 to 0.125
- block_pos: int32 [32], replicated, may hold values from 0 to 31, each once
Outputs:
- layer_out: bfloat16 [2048, 7168], P('head', 'ctx')
The draws below stay inside these ranges and needn't reach their ends.
Inputs may be any that keep to these rules, and one draw needn't show every extreme that they name: Stored block j, rows j * 64 to (j + 1) * 64 - 1, holds the document's block block_pos[j]; every block number appears once.
All inputs are finite; a program needn't handle non-finite values.
Results may differ from the reference program's by a relative error of at most 0.018.
Values may be sent and summed in bfloat16 or wider, within the bound.
A program may use at most 128 MiB of HBM per device.

```python
import math
import jax
import jax.numpy as jnp
from jax import lax

D = 7168
HEADS = 128
KV_RANK = 512
NOPE = 128
ROPE = 64
VDIM = 128
BLK = 64
NBLK = 32
SEQ = 2048


def rope_base(key):
    return jnp.clip(jax.random.normal(key, (SEQ, ROPE), jnp.float32), -3.0, 3.0)


def draw_k_rope(key, part):
    base = rope_base(key)
    values = base
    return values.astype(jnp.bfloat16)


def draw_q_rope(key, part):
    key = jax.random.fold_in(key, 3)
    key_list = jax.random.split(key, 2)
    values = jnp.clip(2.5 * jax.random.normal(key_list[1], (SEQ, HEADS, ROPE), jnp.float32), -15.0, 15.0)
    return values.reshape(SEQ, HEADS * ROPE).astype(jnp.bfloat16)


def draw_latent(key, part):
    key = jax.random.fold_in(key, 11)
    key_list = jax.random.split(key, 3)
    row_scale = jnp.exp(jax.random.uniform(key_list[0], (SEQ, 1), jnp.float32) * math.log(10.0))
    col_scale = jnp.exp(jax.random.uniform(key_list[1], (1, KV_RANK), jnp.float32) * math.log(10.0))
    rough = jnp.clip(jax.random.normal(key_list[2], (SEQ, KV_RANK), jnp.float32), -6.0, 6.0)
    values = rough * row_scale * col_scale
    return (0.25 * values).astype(jnp.bfloat16)


def block_scale(stream_key, extent, cuts, smallest, top_value):
    loudness, own = 1.0, jax.random.fold_in(stream_key, 6)
    for dim, blocks in cuts:
        draws = jnp.exp(jax.random.uniform(jax.random.fold_in(own, dim), (blocks,), jnp.float32, smallest / len(cuts), top_value / len(cuts)))
        loudness = loudness * jnp.repeat(draws, extent[dim] // blocks).reshape([-1 if axis == dim else 1 for axis in range(len(extent))])
    return loudness


def centred(own_key, shape, scale, bound, cuts=(), held_as=jnp.bfloat16):
    loudness = block_scale(own_key, shape, cuts, -0.22, 0.18) if cuts else 1.0
    values = jax.random.normal(own_key, shape, jnp.float32) * scale * loudness
    return jnp.minimum(jnp.maximum(values, -bound), bound).astype(held_as)


def setup_inputs(seed: int = 0) -> dict:
    key_of = jax.random.split(jax.random.key(seed), 10)
    return {
        "q_nope": centred(key_of[0], (SEQ, HEADS * NOPE), 1.5, 9.0, ((0, 16), (1, 8))),
        "q_rope": draw_q_rope(jax.random.fold_in(key_of[9], 71), 0),
        "latent": draw_latent(jax.random.fold_in(key_of[9], 71), 0),
        "k_rope": draw_k_rope(jax.random.fold_in(key_of[9], 71), 0),
        "kv_gain": jnp.clip(jnp.exp(jax.random.uniform(key_of[4], (KV_RANK,), jnp.float32, math.log(0.5), math.log(2.0))), 0.5, 2.0),
        "w_uk": centred(key_of[5], (KV_RANK, HEADS * NOPE), KV_RANK ** -0.5, 0.25, ((1, 8),)),
        "w_uv": centred(key_of[6], (KV_RANK, HEADS * VDIM), KV_RANK ** -0.5, 0.25, ((1, 8),)),
        "w_out": centred(key_of[7], (HEADS * VDIM, D), (HEADS * VDIM // 8) ** -0.5, 0.125, ((0, 8), (1, 16))),
        "block_pos": jax.random.permutation(key_of[8], NBLK).astype(jnp.int32),
    }


def reference(q_nope, q_rope, latent, k_rope, kv_gain, w_uk, w_uv, w_out, block_pos):
    seq_rows = latent.shape[0]
    row_ids = jnp.arange(seq_rows, dtype=jnp.int32)
    positions = block_pos[row_ids // BLK] * BLK + row_ids % BLK
    latent_f = latent.astype(jnp.float32)
    mean_square = lax.optimization_barrier(jnp.mean(latent_f * latent_f, axis=1, keepdims=True))
    normed = (latent_f * lax.rsqrt(mean_square + 1e-06) * kv_gain.astype(jnp.float32)[None, :]).astype(jnp.bfloat16)
    key_nope = jnp.dot(normed, w_uk, preferred_element_type=jnp.float32).astype(jnp.bfloat16)
    values = jnp.dot(normed, w_uv, preferred_element_type=jnp.float32).astype(jnp.bfloat16)
    key_heads = key_nope.reshape(seq_rows, HEADS, NOPE).transpose(1, 0, 2)
    value_heads = values.reshape(seq_rows, HEADS, VDIM).transpose(1, 0, 2)
    query_nope = q_nope.reshape(seq_rows, HEADS, NOPE).transpose(1, 0, 2)
    query_rope = q_rope.reshape(seq_rows, HEADS, ROPE).transpose(1, 0, 2)
    admitted = positions[None, :] <= positions[:, None]
    score_scale = 1.0 / math.sqrt(NOPE + ROPE)

    def one_head(operands):
        head_qn, head_qr, head_kn, head_v = operands
        scores = jnp.dot(head_qn, head_kn.T, preferred_element_type=jnp.float32)
        scores = scores + jnp.dot(head_qr, k_rope.T, preferred_element_type=jnp.float32)
        scores = scores * score_scale
        row_max = lax.optimization_barrier(jnp.max(jnp.where(admitted, scores, -jnp.inf), axis=1))
        expo = jnp.where(admitted, jnp.exp(scores - row_max[:, None]), 0.0)
        row_total = lax.optimization_barrier(jnp.sum(expo, axis=1))
        weights = expo.astype(jnp.bfloat16)
        return jnp.dot(weights, head_v, preferred_element_type=jnp.float32) / row_total[:, None]
    head_out = lax.map(one_head, (query_nope, query_rope, key_heads, value_heads))
    attended = head_out.transpose(1, 0, 2).reshape(seq_rows, HEADS * VDIM).astype(jnp.bfloat16)
    return jnp.dot(attended, w_out, preferred_element_type=jnp.float32).astype(jnp.bfloat16)
```

```python
import functools
import math

import jax
import jax.numpy as jnp
from jax import lax
from jax.experimental import pallas as pl
from jax.experimental.pallas import tpu as pltpu
from jax.sharding import PartitionSpec as P

NOPE = 128
ROPE = 64
VDIM = 128
BLK = 64
FLOOR = -1e30
NT = (((1,), (1,)), ((), ()))
MESH = pl.DeviceIdType.MESH

YS, XS, CORES, ZS, YHS = 2, 4, 2, 4, 2
TO_Y, TO_XP, TO_XM, ON_XP, ON_XM, TO_CORE = 0, 1, 2, 3, 4, 5
GATHER_COPIES = TO_CORE + XS
TO_Z, TO_YH = 0, ZS - 1
SUM_COPIES = ZS


def dot32(a, b):
    return jnp.dot(a, b, preferred_element_type=jnp.float32)


def dot32_nt(a, b):
    return lax.dot_general(a, b, NT, preferred_element_type=jnp.float32)


def layer_kernel(
    heads,
    tokens,
    pos_ref,
    qn_ref,
    qr_ref,
    latent_ref,
    rope_ref,
    gain_ref,
    uk_ref,
    uv_ref,
    wo_ref,
    out_ref,
    kv,
    qa,
    att,
    part,
    zbuf,
    mine,
    ysend,
    ybuf,
    gsend,
    grecv,
    rsend,
    rrecv,
):
    rows = qn_ref.shape[0]
    rank = latent_ref.shape[1]
    width = kv.shape[-1]
    keys = YS * XS * CORES * rows
    chunks = rows // tokens
    exponent = math.log2(math.e) / math.sqrt(NOPE + ROPE)

    ctx = lax.axis_index("ctx")
    head_group = lax.axis_index("head")
    y, x, core = ctx // (XS * CORES), (ctx // CORES) % XS, ctx % CORES
    z, yh = head_group // YHS, head_group % YHS
    x_next, x_last, x_far = (x + 1) % XS, (x + XS - 1) % XS, (x + 2) % XS

    def at_ctx(y_, x_, core_):
        return ((y_ * XS + x_) * CORES + core_, head_group)

    def at_head(z_, yh_):
        return (ctx, z_ * YHS + yh_)

    across = at_ctx(1 - y, x, core)
    ahead = at_ctx(y, x_next, core)
    behind = at_ctx(y, x_last, core)
    sibling = at_ctx(y, x, 1 - core)
    over = at_head(z, 1 - yh)
    above = [at_head((z + k) % ZS, yh) for k in range(1, ZS)]

    barrier = pltpu.get_barrier_semaphore()
    partners = [across, ahead, behind, sibling, over] + above
    for partner in partners:
        pl.semaphore_signal(barrier, inc=1, device_id=partner, device_id_type=MESH)

    def remote(source, target, send, recv, partner):
        return pltpu.make_async_remote_copy(
            src_ref=source,
            dst_ref=target,
            send_sem=send,
            recv_sem=recv,
            device_id=partner,
            device_id_type=MESH,
        )

    def gather_copy(slots, turn, which):
        if which == TO_Y:
            view, partner = slots.at[y, x, core], across
        elif which == TO_XP:
            view, partner = slots.at[:, x, core], ahead
        elif which == TO_XM:
            view, partner = slots.at[:, x, core], behind
        elif which == ON_XP:
            view, partner = slots.at[0, x_last, core], ahead
        elif which == ON_XM:
            view, partner = slots.at[1, x_next, core], behind
        else:
            place = (x, x_last, x_next, x_far)[which - TO_CORE]
            view, partner = slots.at[:, place, core], sibling
        return remote(view, view, gsend.at[turn, which], grecv.at[turn, which], partner)

    def sum_copy(index, which):
        send, recv = rsend.at[index, which], rrecv.at[index, which]
        if which == TO_YH:
            return remote(ysend.at[index], ybuf.at[index], send, recv, over)
        return remote(
            part.at[index, (z + which + 1) % ZS], zbuf.at[index, which], send, recv, above[which]
        )

    def start(slots, turn, *copies):
        for which in copies:
            gather_copy(slots, turn, which).start()

    def arrived(slots, turn, *copies):
        for which in copies:
            gather_copy(slots, turn, which).wait_recv()

    latent = latent_ref[...].astype(jnp.float32)
    mean_square = jnp.mean(latent * latent, axis=1, keepdims=True)
    normed = (latent * lax.rsqrt(mean_square + 1e-06) * gain_ref[...]).astype(jnp.bfloat16)
    kv[y, x, core, :, :rank] = normed
    kv[y, x, core, :, rank:] = jnp.concatenate([rope_ref[...], rope_ref[...]], axis=1)

    pl.semaphore_wait(barrier, len(partners))
    start(kv, chunks, TO_Y)

    lane = lax.broadcasted_iota(jnp.int32, (rows, 2 * ROPE), 1)

    def project(head_list):
        for head in head_list:
            cols = slice(head * NOPE, (head + 1) * NOPE)
            mixed = dot32_nt(qn_ref[:, cols], uk_ref[:, cols]).astype(jnp.bfloat16)
            qa[:, head, :, :rank] = mixed.reshape(chunks, tokens, rank)
            pair = qr_ref[:, (head // 2) * 2 * ROPE : (head // 2 + 1) * 2 * ROPE]
            rope = jnp.where(lane // ROPE == head % 2, pair, jnp.zeros_like(pair))
            qa[:, head, :, rank:] = rope.reshape(chunks, tokens, 2 * ROPE)

    project(range(heads // 2))
    arrived(kv, chunks, TO_Y)
    start(kv, chunks, TO_XP, TO_XM, TO_CORE)
    project(range(heads // 2, heads))

    key_ids = lax.broadcasted_iota(jnp.int32, (tokens, keys), 1)
    key_pos = key_ids % BLK
    for block in range(keys // BLK):
        key_pos = jnp.where(key_ids // BLK == block, key_pos + pos_ref[block] * BLK, key_pos)

    arrived(kv, chunks, TO_XP, TO_XM)
    start(kv, chunks, ON_XP, ON_XM, TO_CORE + 1, TO_CORE + 2)
    arrived(kv, chunks, ON_XP, ON_XM)
    start(kv, chunks, TO_CORE + 3)
    arrived(kv, chunks, *range(TO_CORE, TO_CORE + XS))

    def attend(index):
        first = index * tokens
        first_pos = pos_ref[ctx * (rows // BLK) + first // BLK] * BLK + first % BLK
        query_pos = first_pos + lax.broadcasted_iota(jnp.int32, (tokens, keys), 0)
        bias = jnp.where(key_pos <= query_pos, 0.0, FLOOR)
        scores = dot32_nt(qa[index].reshape(heads * tokens, width), kv[...].reshape(keys, width))
        scores = scores.reshape(heads, tokens, keys) + bias[None]
        top = jnp.max(scores, axis=2, keepdims=True)
        weights = jnp.exp2((scores - top) * exponent)
        total = jnp.sum(weights, axis=2, keepdims=True)
        weights = weights.astype(jnp.bfloat16).reshape(heads * tokens, keys)
        mixed = dot32(weights, kv[:, :, :, :, :rank].reshape(keys, rank))
        mixed = (mixed.reshape(heads, tokens, rank) / total).astype(jnp.bfloat16)
        for head in range(heads):
            cols = slice(head * VDIM, (head + 1) * VDIM)
            att[index, y, x, core, :, cols] = dot32(mixed[head], uv_ref[:, cols]).astype(
                jnp.bfloat16
            )

    def step(turn, carry):
        def stage(delay, body):
            index = turn - delay

            @pl.when(jnp.logical_and(index >= 0, index < chunks))
            def _():
                body(index, att.at[index])

        def across_done(index, slots):
            arrived(slots, index, TO_Y)
            start(slots, index, TO_XP, TO_XM, TO_CORE)

        def along_done(index, slots):
            arrived(slots, index, TO_XP, TO_XM)
            start(slots, index, ON_XP, ON_XM, TO_CORE + 1, TO_CORE + 2)

        def onward_done(index, slots):
            arrived(slots, index, ON_XP, ON_XM)
            start(slots, index, TO_CORE + 3)

        def own(index, slots):
            attend(index)
            start(slots, index, TO_Y)

        def multiply(index, slots):
            arrived(slots, index, *range(TO_CORE, TO_CORE + XS))
            held = att[index].reshape(YS * XS * CORES * tokens, heads * VDIM)
            product = dot32(held, wo_ref[...]).astype(jnp.bfloat16)
            part[index] = product.reshape(ZS, YHS, CORES * tokens, product.shape[1])
            for which in range(ZS - 1):
                sum_copy(index, which).start()

        def sum_z(index, slots):
            for which in range(ZS - 1):
                sum_copy(index, which).wait_recv()

            def summed(half):
                value = part[index, z, half].astype(jnp.float32)
                for which in range(ZS - 1):
                    value += zbuf[index, which, half].astype(jnp.float32)
                return value

            ysend[index] = summed(1 - yh).astype(jnp.bfloat16)
            sum_copy(index, TO_YH).start()
            mine[index] = summed(yh)

        def finish(index, slots):
            sum_copy(index, TO_YH).wait_recv()
            value = (mine[index] + ybuf[index].astype(jnp.float32)).astype(jnp.bfloat16)
            for which in range(CORES):
                place = pl.ds(pl.multiple_of(which * rows + index * tokens, tokens), tokens)
                out_ref[place, :] = value[which * tokens : (which + 1) * tokens]

        stage(3, onward_done)
        stage(2, along_done)
        stage(1, across_done)
        stage(0, own)
        stage(4, multiply)
        stage(5, sum_z)
        stage(6, finish)
        return carry

    lax.fori_loop(0, chunks + 6, step, 0)

    for which in range(GATHER_COPIES):
        gather_copy(kv, chunks, which).wait_send()

    def drain(index, carry):
        for which in range(GATHER_COPIES):
            gather_copy(att.at[index], index, which).wait_send()
        for which in range(SUM_COPIES):
            sum_copy(index, which).wait_send()
        return carry

    lax.fori_loop(0, chunks, drain, 0)


TOKENS = 16


def shards(q_nope, q_rope, latent, k_rope, kv_gain, w_uk, w_uv, w_out, block_pos):
    rows = q_nope.shape[0]
    heads = w_uk.shape[1] // NOPE
    rank = latent.shape[1]
    width = rank + 2 * ROPE
    cols = w_out.shape[1]
    chunks = rows // TOKENS
    vmem = pl.BlockSpec(memory_space=pltpu.VMEM)
    smem = pl.BlockSpec(memory_space=pltpu.SMEM)
    return pl.pallas_call(
        functools.partial(layer_kernel, heads, TOKENS),
        name="layer",
        out_shape=jax.ShapeDtypeStruct((CORES * rows, cols), jnp.bfloat16),
        in_specs=[smem] + [vmem] * 8,
        out_specs=vmem,
        scratch_shapes=[
            pltpu.VMEM((YS, XS, CORES, rows, width), jnp.bfloat16),
            pltpu.VMEM((chunks, heads, TOKENS, width), jnp.bfloat16),
            pltpu.VMEM((chunks, YS, XS, CORES, TOKENS, heads * VDIM), jnp.bfloat16),
            pltpu.VMEM((chunks, ZS, YHS, CORES * TOKENS, cols), jnp.bfloat16),
            pltpu.VMEM((chunks, ZS - 1, YHS, CORES * TOKENS, cols), jnp.bfloat16),
            pltpu.VMEM((chunks, CORES * TOKENS, cols), jnp.float32),
            pltpu.VMEM((chunks, CORES * TOKENS, cols), jnp.bfloat16),
            pltpu.VMEM((chunks, CORES * TOKENS, cols), jnp.bfloat16),
            pltpu.SemaphoreType.DMA((chunks + 1, GATHER_COPIES)),
            pltpu.SemaphoreType.DMA((chunks + 1, GATHER_COPIES)),
            pltpu.SemaphoreType.DMA((chunks, SUM_COPIES)),
            pltpu.SemaphoreType.DMA((chunks, SUM_COPIES)),
        ],
        compiler_params=pltpu.CompilerParams(
            collective_id=0, has_side_effects=True, vmem_limit_bytes=60 * 2**20
        ),
    )(block_pos, q_nope, q_rope, latent, k_rope, kv_gain[None, :], w_uk, w_uv, w_out)


def solution(mesh):
    placed = (
        P("ctx", "head"),
        P("ctx", "head"),
        P("ctx", None),
        P("ctx", None),
        P(),
        P(None, "head"),
        P(None, "head"),
        P("head", "ctx"),
        P(),
    )
    return jax.shard_map(
        shards, mesh=mesh, in_specs=placed, out_specs=P("head", "ctx"), check_vma=False
    )
```

```python
import functools
import math

import jax
import jax.numpy as jnp
from jax import lax
from jax.experimental import pallas as pl
from jax.experimental.pallas import tpu as pltpu
from jax.sharding import PartitionSpec as P

NOPE = 128
ROPE = 64
VDIM = 128
BLK = 64
FLOOR = -1e30
NT = (((1,), (1,)), ((), ()))
MESH = pl.DeviceIdType.MESH

YS, XS, CORES, ZS, YHS = 2, 4, 2, 4, 2
L_FAR, L_FAR_Y, L_XP, L_XM, L_Y1, L_Y2, L_YXP, L_YXM, L_Z, L_CORE = 0, 1, 2, 3, 4, 5, 6, 7, 8, 11
A_Y, A_XP, A_XM, A_ONP, A_ONM, A_CORE = range(6)
B_XP, B_XM, B_ONP, B_ONM, B_Y, B_CORE = 0, 1, 2, 3, 4, 8
LATENT_COPIES = L_CORE + XS
A_COPIES = A_CORE + XS
B_COPIES = B_CORE + YS
GATHER_COPIES = max(A_COPIES, B_COPIES)
B_EVERY, B_FIRST = 3, 2
TO_YH = ZS - 1
SUM_COPIES = ZS
LAST_COPIES = ZS * YHS - 1


def dot32(a, b):
    return jnp.dot(a, b, preferred_element_type=jnp.float32)


def dot32_nt(a, b):
    return lax.dot_general(a, b, NT, preferred_element_type=jnp.float32)


def layer_kernel(
    heads,
    tokens,
    pos_ref,
    qn_hbm,
    qr_hbm,
    latent_ref,
    rope_ref,
    gain_ref,
    uk_hbm,
    uv_hbm,
    wo_hbm,
    out_ref,
    qn_ref,
    qr_ref,
    uk_ref,
    uv_ref,
    wo_ref,
    kv,
    qa,
    att,
    part,
    zbuf,
    mine,
    ysend,
    ybuf,
    lastbuf,
    result,
    load_sem,
    lsend,
    lrecv,
    gsend,
    grecv,
    rsend,
    rrecv,
    fsend,
    frecv,
):
    loads = [
        pltpu.make_async_copy(source, target, load_sem.at[which])
        for which, (source, target) in enumerate(
            [
                (qn_hbm, qn_ref),
                (uk_hbm, uk_ref),
                (qr_hbm, qr_ref),
                (uv_hbm, uv_ref),
                (wo_hbm, wo_ref),
            ]
        )
    ]
    rows = qn_ref.shape[0]
    cols = out_ref.shape[0]
    rank = latent_ref.shape[1]
    width = kv.shape[-1]
    keys = YS * XS * CORES * rows
    chunks = rows // tokens
    exponent = math.log2(math.e) / math.sqrt(NOPE + ROPE)

    ctx = lax.axis_index("ctx")
    head_group = lax.axis_index("head")
    y, x, core = ctx // (XS * CORES), (ctx // CORES) % XS, ctx % CORES
    z, yh = head_group // YHS, head_group % YHS
    x_next, x_last, x_far = (x + 1) % XS, (x + XS - 1) % XS, (x + 2) % XS

    def at_ctx(y_, x_, core_):
        return ((y_ * XS + x_) * CORES + core_, head_group)

    def at_head(z_, yh_):
        return (ctx, z_ * YHS + yh_)

    across = at_ctx(1 - y, x, core)
    ahead = at_ctx(y, x_next, core)
    behind = at_ctx(y, x_last, core)
    sibling = at_ctx(y, x, 1 - core)
    far = at_ctx(y, x_far, core)
    far_across = at_ctx(1 - y, x_far, core)
    across_over = (across[0], at_head(z, 1 - yh)[1])
    others = [(k // YHS, k % YHS) for k in range(1, ZS * YHS)]
    groups = [at_head((z + dz) % ZS, (yh + dy) % YHS) for dz, dy in others]
    over = groups[0]
    above = [groups[YHS * k - 1] for k in range(1, ZS)]

    barrier = pltpu.get_barrier_semaphore()
    partners = [across, ahead, behind, sibling, far, far_across, across_over] + groups
    for partner in partners:
        pl.semaphore_signal(barrier, inc=1, device_id=partner, device_id_type=MESH)

    for load in loads:
        load.start()

    def remote(source, target, send, recv, partner):
        return pltpu.make_async_remote_copy(
            src_ref=source,
            dst_ref=target,
            send_sem=send,
            recv_sem=recv,
            device_id=partner,
            device_id_type=MESH,
        )

    def latent_copy(which):
        half = rows // 2
        own = kv.at[y, x, core]
        quarter = pl.ds(pl.multiple_of(z * (rows // ZS), rows // ZS), rows // ZS)
        if L_Z <= which < L_Z + ZS - 1:
            view, partner = kv.at[:, x_far, core, quarter], above[which - L_Z]
        else:
            view, partner = {
                L_FAR: (own.at[quarter], far),
                L_FAR_Y: (own.at[quarter], far_across),
                L_XP: (own, ahead),
                L_XM: (own, behind),
                L_Y1: (own.at[pl.ds(0, half)], across),
                L_Y2: (own.at[pl.ds(half, half)], across_over),
                L_YXP: (kv.at[1 - y, x, core], ahead),
                L_YXM: (kv.at[1 - y, x, core], behind),
                L_CORE: (kv.at[:, x, core], sibling),
                L_CORE + 1: (kv.at[:, x_last, core], sibling),
                L_CORE + 2: (kv.at[:, x_next, core], sibling),
                L_CORE + 3: (kv.at[:, x_far, core], sibling),
            }[which]
        return remote(view, view, lsend.at[which], lrecv.at[which], partner)

    def a_copy(index, which):
        slots = att.at[index]
        view, partner = {
            A_Y: (slots.at[y, x, core], across),
            A_XP: (slots.at[:, x, core], ahead),
            A_XM: (slots.at[:, x, core], behind),
            A_ONP: (slots.at[0, x_last, core], ahead),
            A_ONM: (slots.at[1, x_next, core], behind),
            A_CORE: (slots.at[:, x, core], sibling),
            A_CORE + 1: (slots.at[:, x_last, core], sibling),
            A_CORE + 2: (slots.at[:, x_next, core], sibling),
            A_CORE + 3: (slots.at[:, x_far, core], sibling),
        }[which]
        return remote(view, view, gsend.at[index, which], grecv.at[index, which], partner)

    def b_copy(index, which):
        slots = att.at[index]
        half = heads * VDIM // 2
        first, second = pl.ds(0, half), pl.ds(half, half)
        view, partner = {
            B_XP: (slots.at[y, x, core], ahead),
            B_XM: (slots.at[y, x, core], behind),
            B_ONP: (slots.at[y, x_last, core, :, first], ahead),
            B_ONM: (slots.at[y, x_next, core, :, second], behind),
            B_Y: (slots.at[y, x, core], across),
            B_Y + 1: (slots.at[y, x_last, core], across),
            B_Y + 2: (slots.at[y, x_next, core], across),
            B_Y + 3: (slots.at[y, x_far, core], across),
            B_CORE: (slots.at[y, :, core], sibling),
            B_CORE + 1: (slots.at[1 - y, :, core], sibling),
        }[which]
        return remote(view, view, gsend.at[index, which], grecv.at[index, which], partner)

    def sum_copy(index, which):
        send, recv = rsend.at[index, which], rrecv.at[index, which]
        if which == TO_YH:
            return remote(ysend.at[index], ybuf.at[index], send, recv, over)
        return remote(
            part.at[index, (z + which + 1) % ZS], zbuf.at[index, which], send, recv, above[which]
        )

    def last_copy(which):
        dz, dy = others[which]
        source = part.at[chunks - 1, (z + dz) % ZS, (yh + dy) % YHS]
        return remote(source, lastbuf.at[which], fsend.at[which], frecv.at[which], groups[which])

    def start(copy, *copies):
        for which in copies:
            copy(which).start()

    def arrived(copy, *copies):
        for which in copies:
            copy(which).wait_recv()

    latent = latent_ref[...].astype(jnp.float32)
    mean_square = jnp.mean(latent * latent, axis=1, keepdims=True)
    normed = (latent * lax.rsqrt(mean_square + 1e-06) * gain_ref[...]).astype(jnp.bfloat16)
    kv[y, x, core, :, :rank] = normed
    rope_key = rope_ref[...].astype(jnp.float32)
    rope_key = jnp.concatenate([rope_key, rope_key], axis=0).T
    kv[y, x, core, :, rank:] = rope_key.astype(jnp.bfloat16)

    lane = lax.broadcasted_iota(jnp.int32, (rows, 2 * ROPE), 1)

    def project(head_list):
        for head in head_list:
            span = slice(head * NOPE, (head + 1) * NOPE)
            mixed = dot32_nt(qn_ref[:, span], uk_ref[:, span]).astype(jnp.bfloat16)
            qa[:, head, :, :rank] = mixed.reshape(chunks, tokens, rank)
            pair = qr_ref[:, (head // 2) * 2 * ROPE : (head // 2 + 1) * 2 * ROPE]
            rope = jnp.where(lane // ROPE == head % 2, pair, jnp.zeros_like(pair))
            qa[:, head, :, rank:] = rope.reshape(chunks, tokens, 2 * ROPE)

    for load in loads[:3]:
        load.wait()
    project(range(heads // 2))
    pl.semaphore_wait(barrier, len(partners))
    start(latent_copy, L_FAR, L_FAR_Y, L_XP, L_XM, L_Y1, L_Y2)
    project(range(heads // 2, heads))

    key_ids = lax.broadcasted_iota(jnp.int32, (1, keys), 1)
    key_pos = key_ids % BLK
    for block in range(keys // BLK):
        key_pos = jnp.where(key_ids // BLK == block, key_pos + pos_ref[block] * BLK, key_pos)

    arrived(latent_copy, L_Y1, L_Y2)
    start(latent_copy, L_YXP, L_YXM)
    arrived(latent_copy, L_FAR, L_FAR_Y)
    start(latent_copy, L_Z, L_Z + 1, L_Z + 2, L_CORE)
    for load in loads[3:]:
        load.wait()
    arrived(latent_copy, L_XP, L_XM, L_YXP, L_YXM)
    start(latent_copy, L_CORE + 1, L_CORE + 2)
    arrived(latent_copy, L_Z, L_Z + 1, L_Z + 2)
    start(latent_copy, L_CORE + 3)
    arrived(latent_copy, *range(L_CORE, L_CORE + XS))

    def attend(index):
        first = index * tokens
        first_pos = pos_ref[ctx * (rows // BLK) + first // BLK] * BLK + first % BLK
        query_pos = first_pos + lax.broadcasted_iota(jnp.int32, (tokens, 1), 0)
        bias = jnp.where(key_pos <= query_pos, 0.0, FLOOR)
        scores = dot32_nt(qa[index].reshape(heads * tokens, width), kv[...].reshape(keys, width))
        scores = scores.reshape(heads, tokens, keys) + bias[None]
        top = jnp.max(scores, axis=2, keepdims=True)
        weights = jnp.exp2((scores - top) * exponent)
        total = jnp.sum(weights, axis=2, keepdims=True)
        weights = weights.astype(jnp.bfloat16).reshape(heads * tokens, keys)
        mixed = dot32(weights, kv[:, :, :, :, :rank].reshape(keys, rank))
        mixed = (mixed.reshape(heads, tokens, rank) / total).astype(jnp.bfloat16)
        for head in range(heads):
            span = slice(head * VDIM, (head + 1) * VDIM)
            att[index, y, x, core, :, span] = dot32(mixed[head], uv_ref[:, span]).astype(
                jnp.bfloat16
            )

    def a_own(index, copy):
        start(copy, A_Y)

    def a_across(index, copy):
        arrived(copy, A_Y)
        start(copy, A_XP, A_XM, A_CORE)

    def a_along(index, copy):
        arrived(copy, A_XP, A_XM)
        start(copy, A_ONP, A_ONM, A_CORE + 1, A_CORE + 2)

    def a_onward(index, copy):
        arrived(copy, A_ONP, A_ONM)
        start(copy, A_CORE + 3)

    def a_all(index, copy):
        arrived(copy, *range(A_CORE, A_CORE + XS))

    def b_own(index, copy):
        start(copy, B_XP, B_XM, B_Y)

    def b_along(index, copy):
        arrived(copy, B_XP, B_XM)
        start(copy, B_ONP, B_ONM, B_Y + 1, B_Y + 2)

    def b_onward(index, copy):
        arrived(copy, B_ONP, B_ONM)
        start(copy, B_Y + 3, B_CORE)

    def b_across(index, copy):
        arrived(copy, *range(B_Y, B_Y + XS))
        start(copy, B_CORE + 1)

    def b_all(index, copy):
        arrived(copy, *range(B_CORE, B_CORE + YS))

    def own(index, copy):
        attend(index)

    def multiply(index, copy):
        held = att[index].reshape(YS * XS * CORES * tokens, heads * VDIM)
        product = dot32_nt(held, wo_ref[...]).astype(jnp.bfloat16)
        part[index] = product.reshape(ZS, YHS, CORES * tokens, cols)
        if isinstance(index, int) and index == chunks - 1:
            start(last_copy, *range(LAST_COPIES))
        else:
            start(functools.partial(sum_copy, index), *range(ZS - 1))

    def sum_z(index, copy):
        for which in range(ZS - 1):
            sum_copy(index, which).wait_recv()

        def summed(half):
            value = part[index, z, half].astype(jnp.float32)
            for which in range(ZS - 1):
                value += zbuf[index, which, half].astype(jnp.float32)
            return value

        ysend[index] = summed(1 - yh).astype(jnp.bfloat16)
        sum_copy(index, TO_YH).start()
        mine[index] = summed(yh)

    def finish(index, copy):
        sum_copy(index, TO_YH).wait_recv()
        value = mine[index] + ybuf[index].astype(jnp.float32)
        place_rows(index, value)

    def place_rows(index, value):
        for which in range(CORES):
            place = pl.ds(pl.multiple_of(which * rows + index * tokens, tokens), tokens)
            result[place, :cols] = value[which * tokens : (which + 1) * tokens]

    def finish_last():
        arrived(last_copy, *range(LAST_COPIES))
        value = part[chunks - 1, z, yh].astype(jnp.float32)
        for which in range(LAST_COPIES):
            value += lastbuf[which].astype(jnp.float32)
        place_rows(chunks - 1, value)

    def sent(index):
        is_b = index % B_EVERY == B_FIRST
        copy = functools.partial(b_copy if is_b else a_copy, index)
        for which in range(B_COPIES if is_b else A_COPIES):
            copy(which).wait_send()
        for which in range(SUM_COPIES if index < chunks - 1 else 0):
            sum_copy(index, which).wait_send()

    def step(turn, carry):
        def stage(delay, body, kind=None):
            index = turn - delay
            due = index >= 0
            if kind is not None:
                due = jnp.logical_and(due, (index % B_EVERY == B_FIRST) == kind)

            @pl.when(due)
            def _():
                body(index, functools.partial(b_copy if kind else a_copy, index))

        stage(0, own)
        stage(0, a_own, False)
        stage(0, b_own, True)
        stage(1, a_across, False)
        stage(3, a_along, False)
        stage(3, b_along, True)
        stage(5, a_onward, False)
        stage(5, b_onward, True)
        stage(6, b_across, True)
        stage(6, a_all, False)
        stage(6, b_all, True)
        stage(6, multiply)
        stage(7, sum_z)
        return carry

    lax.fori_loop(0, chunks, step, 0)

    rest = [
        (b_along, 5),
        (a_onward, 3),
        (a_across, 7),
        (b_across, 2),
        (a_all, 3),
        (multiply, 3),
        (a_along, 6),
        (finish, 0),
        (a_onward, 4),
        (b_all, 2),
        (multiply, 2),
        (b_onward, 5),
        (sum_z, 1),
        (a_all, 4),
        (multiply, 4),
        (a_along, 7),
        (sum_z, 3),
        (b_across, 5),
        (a_onward, 6),
        (finish, 1),
        (sum_z, 2),
        (b_all, 5),
        (multiply, 5),
        (a_onward, 7),
        (finish, 3),
        (a_all, 6),
        (multiply, 6),
        (sum_z, 4),
        (a_all, 7),
        (multiply, 7),
        (finish, 2),
        (sum_z, 5),
        (finish, 4),
        (sum_z, 6),
        (finish, 5),
        (finish, 6),
    ]
    for body, index in rest:
        is_b = index % B_EVERY == B_FIRST
        body(index, functools.partial(b_copy if is_b else a_copy, index))
    for which in range(LATENT_COPIES):
        latent_copy(which).wait_send()
    for index in range(chunks):
        sent(index)
    finish_last()
    out_ref[...] = result[...].T[:cols].astype(jnp.bfloat16)
    for which in range(LAST_COPIES):
        last_copy(which).wait_send()


TOKENS = 16


def shards(q_nope, q_rope, latent, k_rope, kv_gain, w_uk, w_uv, w_out, block_pos):
    rows = q_nope.shape[0]
    heads = w_uk.shape[1] // NOPE
    rank = latent.shape[1]
    width = rank + 2 * ROPE
    cols = w_out.shape[1]
    chunks = rows // TOKENS
    vmem = pl.BlockSpec(memory_space=pltpu.VMEM)
    smem = pl.BlockSpec(memory_space=pltpu.SMEM)
    hbm = pl.BlockSpec(memory_space=pl.ANY)
    return pl.pallas_call(
        functools.partial(layer_kernel, heads, TOKENS),
        name="layer",
        out_shape=jax.ShapeDtypeStruct((cols, CORES * rows), jnp.bfloat16),
        in_specs=[smem, hbm, hbm, vmem, vmem, vmem, hbm, hbm, hbm],
        out_specs=vmem,
        scratch_shapes=[
            pltpu.VMEM(q_nope.shape, q_nope.dtype),
            pltpu.VMEM(q_rope.shape, q_rope.dtype),
            pltpu.VMEM(w_uk.shape, w_uk.dtype),
            pltpu.VMEM(w_uv.shape, w_uv.dtype),
            pltpu.VMEM((cols, heads * VDIM), w_out.dtype),
            pltpu.VMEM((YS, XS, CORES, rows, width), jnp.bfloat16),
            pltpu.VMEM((chunks, heads, TOKENS, width), jnp.bfloat16),
            pltpu.VMEM((chunks, YS, XS, CORES, TOKENS, heads * VDIM), jnp.bfloat16),
            pltpu.VMEM((chunks, ZS, YHS, CORES * TOKENS, cols), jnp.bfloat16),
            pltpu.VMEM((chunks, ZS - 1, YHS, CORES * TOKENS, cols), jnp.bfloat16),
            pltpu.VMEM((chunks, CORES * TOKENS, cols), jnp.float32),
            pltpu.VMEM((chunks, CORES * TOKENS, cols), jnp.bfloat16),
            pltpu.VMEM((chunks, CORES * TOKENS, cols), jnp.bfloat16),
            pltpu.VMEM((LAST_COPIES, CORES * TOKENS, cols), jnp.bfloat16),
            pltpu.VMEM((CORES * rows, pl.cdiv(cols, 128) * 128), jnp.float32),
            pltpu.SemaphoreType.DMA((5,)),
            pltpu.SemaphoreType.DMA((LATENT_COPIES,)),
            pltpu.SemaphoreType.DMA((LATENT_COPIES,)),
            pltpu.SemaphoreType.DMA((chunks, GATHER_COPIES)),
            pltpu.SemaphoreType.DMA((chunks, GATHER_COPIES)),
            pltpu.SemaphoreType.DMA((chunks, SUM_COPIES)),
            pltpu.SemaphoreType.DMA((chunks, SUM_COPIES)),
            pltpu.SemaphoreType.DMA((LAST_COPIES,)),
            pltpu.SemaphoreType.DMA((LAST_COPIES,)),
        ],
        compiler_params=pltpu.CompilerParams(
            collective_id=0, has_side_effects=True, vmem_limit_bytes=60 * 2**20
        ),
    )(block_pos, q_nope, q_rope, latent, k_rope.T, kv_gain[None, :], w_uk, w_uv, w_out.T).T


def solution(mesh):
    placed = (
        P("ctx", "head"),
        P("ctx", "head"),
        P("ctx", None),
        P("ctx", None),
        P(),
        P(None, "head"),
        P(None, "head"),
        P("head", "ctx"),
        P(),
    )
    return jax.shard_map(
        shards, mesh=mesh, in_specs=placed, out_specs=P("head", "ctx"), check_vma=False
    )
```

```python
import functools
import math

import jax
import jax.numpy as jnp
from jax import lax
from jax.experimental import pallas as pl
from jax.experimental.pallas import tpu as pltpu
from jax.sharding import PartitionSpec as P

NOPE = 128
ROPE = 64
VDIM = 128
BLK = 64
FLOOR = -1e30
NT = (((1,), (1,)), ((), ()))
MESH = pl.DeviceIdType.MESH

YS, XS, CORES, ZS, YHS = 2, 4, 2, 4, 2
L_FAR, L_FAR_Y, L_XP, L_XM, L_Y1, L_Y2, L_YXP, L_YXM, L_Z, L_CORE = 0, 1, 2, 3, 4, 5, 6, 7, 8, 11
A_Y, A_XP, A_XM, A_ONP, A_ONM, A_CORE = range(6)
B_XP, B_XM, B_ONP, B_ONM, B_Y, B_CORE = 0, 1, 2, 3, 4, 8
LATENT_COPIES = L_CORE + 6
A_COPIES = A_CORE + XS
B_COPIES = B_CORE + YS
GATHER_COPIES = max(A_COPIES, B_COPIES)
X_FIRST = (1, 3, 5)
TO_YH = ZS - 1
SUM_COPIES = ZS
LAST_COPIES = ZS * YHS - 1


def dot32(a, b):
    return jnp.dot(a, b, preferred_element_type=jnp.float32)


def dot32_nt(a, b):
    return lax.dot_general(a, b, NT, preferred_element_type=jnp.float32)


def layer_kernel(
    heads,
    tokens,
    pos_hbm,
    qn_hbm,
    qr_hbm,
    latent_hbm,
    rope_hbm,
    gain_hbm,
    uk_hbm,
    uv_hbm,
    wo_hbm,
    out_ref,
    pos_ref,
    latent_ref,
    rope_ref,
    gain_ref,
    qn_ref,
    qr_ref,
    uk_ref,
    uv_ref,
    wo_ref,
    kv,
    qa,
    att,
    part,
    zbuf,
    mine,
    ysend,
    ybuf,
    last_part,
    lastbuf,
    result,
    load_sem,
    lsend,
    lrecv,
    gsend,
    grecv,
    rsend,
    rrecv,
    fsend,
    frecv,
    greeted,
):
    rows = qn_ref.shape[0]
    cols = out_ref.shape[0]
    rank = latent_ref.shape[1]
    width = kv.shape[-1]
    keys = YS * XS * CORES * rows
    chunks = rows // tokens
    exponent = math.log2(math.e) / math.sqrt(NOPE + ROPE)

    ctx = lax.axis_index("ctx")
    head_group = lax.axis_index("head")
    y, x, core = ctx // (XS * CORES), (ctx // CORES) % XS, ctx % CORES
    z, yh = head_group // YHS, head_group % YHS
    x_next, x_last, x_far = (x + 1) % XS, (x + XS - 1) % XS, (x + 2) % XS

    def at_ctx(y_, x_, core_):
        return ((y_ * XS + x_) * CORES + core_, head_group)

    def at_head(z_, yh_):
        return (ctx, z_ * YHS + yh_)

    across = at_ctx(1 - y, x, core)
    ahead = at_ctx(y, x_next, core)
    behind = at_ctx(y, x_last, core)
    sibling = at_ctx(y, x, 1 - core)
    far = at_ctx(y, x_far, core)
    far_across = at_ctx(1 - y, x_far, core)
    across_over = (across[0], at_head(z, 1 - yh)[1])
    others = [(k // YHS, k % YHS) for k in range(1, ZS * YHS)]
    groups = [at_head((z + dz) % ZS, (yh + dy) % YHS) for dz, dy in others]
    over = groups[0]
    above = [groups[YHS * k - 1] for k in range(1, ZS)]

    barrier = pltpu.get_barrier_semaphore()
    partners = [across, ahead, behind, sibling, far, far_across, across_over, above[0], above[2]]
    for partner in partners:
        pl.semaphore_signal(barrier, inc=1, device_id=partner, device_id_type=MESH)

    loads = [
        pltpu.make_async_copy(source, target, load_sem.at[which])
        for which, (source, target) in enumerate(
            [
                (latent_hbm, latent_ref),
                (gain_hbm, gain_ref),
                (rope_hbm, rope_ref),
                (qn_hbm, qn_ref),
                (uk_hbm, uk_ref),
                (qr_hbm, qr_ref),
                (pos_hbm, pos_ref),
                (uv_hbm, uv_ref),
                (wo_hbm, wo_ref),
            ]
        )
    ]
    for load in loads:
        load.start()

    def remote(source, target, send, recv, partner):
        return pltpu.make_async_remote_copy(
            src_ref=source,
            dst_ref=target,
            send_sem=send,
            recv_sem=recv,
            device_id=partner,
            device_id_type=MESH,
        )

    def latent_copy(which):
        half = rows // 2
        own = kv.at[y, x, core]
        quarter = pl.ds(pl.multiple_of(z * (rows // ZS), rows // ZS), rows // ZS)
        if L_Z <= which < L_Z + ZS - 1:
            view, partner = kv.at[:, x_far, core, quarter], above[which - L_Z]
        else:
            view, partner = {
                L_FAR: (own.at[quarter], far),
                L_FAR_Y: (own.at[quarter], far_across),
                L_XP: (own, ahead),
                L_XM: (own, behind),
                L_Y1: (own.at[pl.ds(0, half)], across),
                L_Y2: (own.at[pl.ds(half, half)], across_over),
                L_YXP: (kv.at[1 - y, x, core], ahead),
                L_YXM: (kv.at[1 - y, x, core], behind),
                L_CORE: (kv.at[:, x, core], sibling),
                L_CORE + 1: (kv.at[y, x_last, core], sibling),
                L_CORE + 2: (kv.at[y, x_next, core], sibling),
                L_CORE + 3: (kv.at[:, x_far, core], sibling),
                L_CORE + 4: (kv.at[1 - y, x_last, core], sibling),
                L_CORE + 5: (kv.at[1 - y, x_next, core], sibling),
            }[which]
        return remote(view, view, lsend.at[which], lrecv.at[which], partner)

    def a_copy(index, which):
        slots = att.at[index]
        view, partner = {
            A_Y: (slots.at[y, x, core], across),
            A_XP: (slots.at[:, x, core], ahead),
            A_XM: (slots.at[:, x, core], behind),
            A_ONP: (slots.at[0, x_last, core], ahead),
            A_ONM: (slots.at[1, x_next, core], behind),
            A_CORE: (slots.at[:, x, core], sibling),
            A_CORE + 1: (slots.at[:, x_last, core], sibling),
            A_CORE + 2: (slots.at[:, x_next, core], sibling),
            A_CORE + 3: (slots.at[:, x_far, core], sibling),
        }[which]
        return remote(view, view, gsend.at[index, which], grecv.at[index, which], partner)

    def b_copy(index, which):
        slots = att.at[index]
        half = heads * VDIM // 2
        first, second = pl.ds(0, half), pl.ds(half, half)
        view, partner = {
            B_XP: (slots.at[y, x, core], ahead),
            B_XM: (slots.at[y, x, core], behind),
            B_ONP: (slots.at[y, x_last, core, :, first], ahead),
            B_ONM: (slots.at[y, x_next, core, :, second], behind),
            B_Y: (slots.at[y, x, core], across),
            B_Y + 1: (slots.at[y, x_last, core], across),
            B_Y + 2: (slots.at[y, x_next, core], across),
            B_Y + 3: (slots.at[y, x_far, core], across),
            B_CORE: (slots.at[y, :, core], sibling),
            B_CORE + 1: (slots.at[1 - y, :, core], sibling),
        }[which]
        return remote(view, view, gsend.at[index, which], grecv.at[index, which], partner)

    def sum_copy(index, which):
        send, recv = rsend.at[index, which], rrecv.at[index, which]
        if which == TO_YH:
            return remote(ysend.at[index], ybuf.at[index], send, recv, over)
        return remote(
            part.at[index, (z + which + 1) % ZS], zbuf.at[index, which], send, recv, above[which]
        )

    def last_copy(which):
        dz, dy = others[which]
        source = last_part.at[(z + dz) % ZS, (yh + dy) % YHS]
        return remote(source, lastbuf.at[which], fsend.at[which], frecv.at[which], groups[which])

    def start(copy, *copies):
        for which in copies:
            copy(which).start()

    def arrived(copy, *copies):
        for which in copies:
            copy(which).wait_recv()

    for load in loads[:3]:
        load.wait()
    latent = latent_ref[...].astype(jnp.float32)
    mean_square = jnp.mean(latent * latent, axis=1, keepdims=True)
    normed = (latent * lax.rsqrt(mean_square + 1e-06) * gain_ref[...]).astype(jnp.bfloat16)
    kv[y, x, core, :, :rank] = normed
    rope_key = rope_ref[...].astype(jnp.float32)
    rope_key = jnp.concatenate([rope_key, rope_key], axis=0).T
    kv[y, x, core, :, rank:] = rope_key.astype(jnp.bfloat16)

    lane = lax.broadcasted_iota(jnp.int32, (rows, 2 * ROPE), 1)

    def project(head_list):
        for head in head_list:
            span = slice(head * NOPE, (head + 1) * NOPE)
            mixed = dot32_nt(qn_ref[:, span], uk_ref[:, span]).astype(jnp.bfloat16)
            qa[:, head, :, :rank] = mixed.reshape(chunks, tokens, rank)
            pair = qr_ref[:, (head // 2) * 2 * ROPE : (head // 2 + 1) * 2 * ROPE]
            rope = jnp.where(lane // ROPE == head % 2, pair, jnp.zeros_like(pair))
            qa[:, head, :, rank:] = rope.reshape(chunks, tokens, 2 * ROPE)

    for load in loads[3:7]:
        load.wait()
    project(range(heads // 2))
    pl.semaphore_wait(barrier, len(partners))
    start(latent_copy, L_FAR, L_FAR_Y, L_XP, L_XM, L_Y1, L_Y2)
    for neighbour in (above[0], above[2]):
        pl.semaphore_signal(greeted, inc=1, device_id=neighbour, device_id_type=MESH)
    project(range(heads // 2, heads))

    key_ids = lax.broadcasted_iota(jnp.int32, (1, keys), 1)
    key_pos = key_ids % BLK
    for block in range(keys // BLK):
        key_pos = jnp.where(key_ids // BLK == block, key_pos + pos_ref[block] * BLK, key_pos)

    arrived(latent_copy, L_Y1, L_Y2)
    start(latent_copy, L_YXP, L_YXM)
    arrived(latent_copy, L_FAR, L_FAR_Y)
    pl.semaphore_wait(greeted, 2)
    start(latent_copy, L_Z, L_Z + 1, L_Z + 2, L_CORE)
    for load in loads[7:]:
        load.wait()
    arrived(latent_copy, L_XP, L_XM)
    start(latent_copy, L_CORE + 1, L_CORE + 2)
    arrived(latent_copy, L_YXP, L_YXM)
    start(latent_copy, L_CORE + 4, L_CORE + 5)
    arrived(latent_copy, L_Z, L_Z + 1, L_Z + 2)
    start(latent_copy, L_CORE + 3)
    arrived(latent_copy, *range(L_CORE, LATENT_COPIES))

    def attend(index):
        first = index * tokens
        first_pos = pos_ref[ctx * (rows // BLK) + first // BLK] * BLK + first % BLK
        query_pos = first_pos + lax.broadcasted_iota(jnp.int32, (tokens, 1), 0)
        bias = jnp.where(key_pos <= query_pos, 0.0, FLOOR)
        scores = dot32_nt(qa[index].reshape(heads * tokens, width), kv[...].reshape(keys, width))
        scores = scores.reshape(heads, tokens, keys) + bias[None]
        top = jnp.max(scores, axis=2, keepdims=True)
        weights = jnp.exp2((scores - top) * exponent)
        total = jnp.sum(weights, axis=2, keepdims=True)
        weights = weights.astype(jnp.bfloat16).reshape(heads * tokens, keys)
        mixed = dot32(weights, kv[:, :, :, :, :rank].reshape(keys, rank))
        mixed = (mixed.reshape(heads, tokens, rank) / total).astype(jnp.bfloat16)
        for head in range(heads):
            span = slice(head * VDIM, (head + 1) * VDIM)
            att[index, y, x, core, :, span] = dot32(mixed[head], uv_ref[:, span]).astype(
                jnp.bfloat16
            )

    def a_own(index, copy):
        start(copy, A_Y)

    def a_across(index, copy):
        arrived(copy, A_Y)
        start(copy, A_XP, A_XM, A_CORE)

    def a_along(index, copy):
        arrived(copy, A_XP, A_XM)
        start(copy, A_ONP, A_ONM, A_CORE + 1, A_CORE + 2)

    def a_onward(index, copy):
        arrived(copy, A_ONP, A_ONM)
        start(copy, A_CORE + 3)

    def a_all(index, copy):
        arrived(copy, *range(A_CORE, A_CORE + XS))

    def b_own(index, copy):
        start(copy, B_XP, B_XM, B_Y)

    def b_along(index, copy):
        arrived(copy, B_XP, B_XM)
        start(copy, B_ONP, B_ONM, B_Y + 1, B_Y + 2)

    def b_onward(index, copy):
        arrived(copy, B_ONP, B_ONM)
        start(copy, B_Y + 3, B_CORE)

    def b_across(index, copy):
        arrived(copy, *range(B_Y, B_Y + XS))
        start(copy, B_CORE + 1)

    def b_all(index, copy):
        arrived(copy, *range(B_CORE, B_CORE + YS))

    def multiply(index, copy):
        held = att[index].reshape(YS * XS * CORES * tokens, heads * VDIM)
        product = dot32_nt(held, wo_ref[...]).astype(jnp.bfloat16)
        product = product.reshape(ZS, YHS, CORES * tokens, cols)
        if isinstance(index, int) and index == chunks - 1:
            last_part[...] = product
            start(last_copy, *range(LAST_COPIES))
        else:
            part[index] = jnp.concatenate([product[:, 0], product[:, 1]], axis=2)
            start(functools.partial(sum_copy, index), *range(ZS - 1))

    def sum_z(index, copy):
        for which in range(ZS - 1):
            sum_copy(index, which).wait_recv()

        value = part[index, z].astype(jnp.float32)
        for which in range(ZS - 1):
            value += zbuf[index, which].astype(jnp.float32)
        lower, upper = value[:, :cols], value[:, cols:]
        ysend[index] = jnp.where(yh == 0, upper, lower).astype(jnp.bfloat16)
        sum_copy(index, TO_YH).start()
        mine[index] = jnp.where(yh == 0, lower, upper)

    def finish(index, copy):
        sum_copy(index, TO_YH).wait_recv()
        value = mine[index] + ybuf[index].astype(jnp.float32)
        place_rows(index, value)

    def place_rows(index, value):
        for which in range(CORES):
            place = pl.ds(pl.multiple_of(which * rows + index * tokens, tokens), tokens)
            result[place, :cols] = value[which * tokens : (which + 1) * tokens]

    def finish_last():
        arrived(last_copy, *range(LAST_COPIES))
        value = last_part[z, yh].astype(jnp.float32)
        for which in range(LAST_COPIES):
            value += lastbuf[which].astype(jnp.float32)
        place_rows(chunks - 1, value)

    def sent(index):
        is_b = index in X_FIRST
        copy = functools.partial(b_copy if is_b else a_copy, index)
        for which in range(B_COPIES if is_b else A_COPIES):
            copy(which).wait_send()
        for which in range(SUM_COPIES if index < chunks - 1 else 0):
            sum_copy(index, which).wait_send()

    def step(turn, carry):
        def stage(body, taken):
            index = -1
            for round_, chunk in enumerate(taken):
                if chunk >= 0:
                    index = jnp.where(turn == round_, chunk, index)

            @pl.when(index >= 0)
            def _():
                copy = b_copy if body.__name__.startswith("b_") else a_copy
                body(index, functools.partial(copy, index))

        attend(turn)
        stage(a_own, [-1 if k in X_FIRST else k for k in range(chunks)])
        stage(b_own, [k if k in X_FIRST else -1 for k in range(chunks)])
        stage(a_across, [-1, -1, 0, -1, 2, -1, 4, -1])
        stage(b_onward, [-1, -1, -1, -1, -1, 1, -1, 3])
        stage(a_along, [-1, -1, -1, -1, 0, -1, 2, -1])
        stage(b_across, [-1, -1, -1, -1, -1, -1, -1, 1])
        stage(b_along, [-1, -1, -1, 1, -1, 3, -1, 5])
        stage(a_onward, [-1, -1, -1, -1, -1, -1, 0, -1])
        return carry

    lax.fori_loop(0, chunks, step, 0)

    rest = [
        (a_all, 0),
        (multiply, 0),
        (a_along, 4),
        (b_all, 1),
        (multiply, 1),
        (a_across, 6),
        (a_onward, 2),
        (b_onward, 5),
        (a_across, 7),
        (sum_z, 0),
        (a_onward, 4),
        (a_all, 2),
        (multiply, 2),
        (b_across, 3),
        (a_all, 4),
        (multiply, 4),
        (sum_z, 1),
        (a_along, 6),
        (b_all, 3),
        (multiply, 3),
        (b_across, 5),
        (sum_z, 2),
        (finish, 0),
        (a_along, 7),
        (finish, 1),
        (b_all, 5),
        (multiply, 5),
        (a_onward, 6),
        (sum_z, 4),
        (finish, 2),
        (a_onward, 7),
        (a_all, 6),
        (multiply, 6),
        (sum_z, 3),
        (a_all, 7),
        (multiply, 7),
        (finish, 4),
        (sum_z, 5),
        (finish, 3),
        (sum_z, 6),
        (finish, 5),
        (finish, 6),
    ]
    for body, index in rest:
        body(index, functools.partial(b_copy if index in X_FIRST else a_copy, index))
    for which in range(LATENT_COPIES):
        latent_copy(which).wait_send()
    for index in range(chunks):
        sent(index)
    finish_last()
    out_ref[...] = result[...].T[:cols].astype(jnp.bfloat16)
    for which in range(LAST_COPIES):
        last_copy(which).wait_send()


TOKENS = 16


def shards(q_nope, q_rope, latent, k_rope, kv_gain, w_uk, w_uv, w_out, block_pos):
    rows = q_nope.shape[0]
    heads = w_uk.shape[1] // NOPE
    rank = latent.shape[1]
    width = rank + 2 * ROPE
    cols = w_out.shape[1]
    chunks = rows // TOKENS
    vmem = pl.BlockSpec(memory_space=pltpu.VMEM)
    hbm = pl.BlockSpec(memory_space=pl.ANY)
    return pl.pallas_call(
        functools.partial(layer_kernel, heads, TOKENS),
        name="layer",
        out_shape=jax.ShapeDtypeStruct((cols, CORES * rows), jnp.bfloat16),
        in_specs=[hbm] * 9,
        out_specs=vmem,
        scratch_shapes=[
            pltpu.SMEM(block_pos.shape, block_pos.dtype),
            pltpu.VMEM(latent.shape, latent.dtype),
            pltpu.VMEM(k_rope.shape[::-1], k_rope.dtype),
            pltpu.VMEM((1, rank), kv_gain.dtype),
            pltpu.VMEM(q_nope.shape, q_nope.dtype),
            pltpu.VMEM(q_rope.shape, q_rope.dtype),
            pltpu.VMEM(w_uk.shape, w_uk.dtype),
            pltpu.VMEM(w_uv.shape, w_uv.dtype),
            pltpu.VMEM((cols, heads * VDIM), w_out.dtype),
            pltpu.VMEM((YS, XS, CORES, rows, width), jnp.bfloat16),
            pltpu.VMEM((chunks, heads, TOKENS, width), jnp.bfloat16),
            pltpu.VMEM((chunks, YS, XS, CORES, TOKENS, heads * VDIM), jnp.bfloat16),
            pltpu.VMEM((chunks, ZS, CORES * TOKENS, YHS * cols), jnp.bfloat16),
            pltpu.VMEM((chunks, ZS - 1, CORES * TOKENS, YHS * cols), jnp.bfloat16),
            pltpu.VMEM((chunks, CORES * TOKENS, cols), jnp.float32),
            pltpu.VMEM((chunks, CORES * TOKENS, cols), jnp.bfloat16),
            pltpu.VMEM((chunks, CORES * TOKENS, cols), jnp.bfloat16),
            pltpu.VMEM((ZS, YHS, CORES * TOKENS, cols), jnp.bfloat16),
            pltpu.VMEM((LAST_COPIES, CORES * TOKENS, cols), jnp.bfloat16),
            pltpu.VMEM((CORES * rows, pl.cdiv(cols, 128) * 128), jnp.float32),
            pltpu.SemaphoreType.DMA((9,)),
            pltpu.SemaphoreType.DMA((LATENT_COPIES,)),
            pltpu.SemaphoreType.DMA((LATENT_COPIES,)),
            pltpu.SemaphoreType.DMA((chunks, GATHER_COPIES)),
            pltpu.SemaphoreType.DMA((chunks, GATHER_COPIES)),
            pltpu.SemaphoreType.DMA((chunks, SUM_COPIES)),
            pltpu.SemaphoreType.DMA((chunks, SUM_COPIES)),
            pltpu.SemaphoreType.DMA((LAST_COPIES,)),
            pltpu.SemaphoreType.DMA((LAST_COPIES,)),
            pltpu.SemaphoreType.REGULAR,
        ],
        compiler_params=pltpu.CompilerParams(
            collective_id=0, has_side_effects=True, vmem_limit_bytes=60 * 2**20
        ),
    )(block_pos, q_nope, q_rope, latent, k_rope.T, kv_gain[None, :], w_uk, w_uv, w_out.T).T


def solution(mesh):
    placed = (
        P("ctx", "head"),
        P("ctx", "head"),
        P("ctx", None),
        P("ctx", None),
        P(),
        P(None, "head"),
        P(None, "head"),
        P("head", "ctx"),
        P(),
    )
    return jax.shard_map(
        shards, mesh=mesh, in_specs=placed, out_specs=P("head", "ctx"), check_vma=False
    )
```

```python
import functools
import math

import jax
import jax.numpy as jnp
from jax import lax
from jax.experimental import pallas as pl
from jax.experimental.pallas import tpu as pltpu
from jax.sharding import PartitionSpec as P

NOPE = 128
ROPE = 64
VDIM = 128
BLK = 64
FLOOR = -1e30
NT = (((1,), (1,)), ((), ()))
MESH = pl.DeviceIdType.MESH

YS, XS, CORES, ZS, YHS = 2, 4, 2, 4, 2
SLOTS = ((0, 0), (1, 0), (0, 3), (0, 1), (1, 3), (1, 1), (0, 2), (1, 2))
PACKED = 16
L_FAR, L_FAR_Y, L_XP, L_XM, L_Y1, L_Y2, L_YXP, L_YXM, L_Z, L_CORE = 0, 1, 2, 3, 4, 5, 6, 7, 8, 11
A_Y, A_XP, A_XM, A_ONP, A_ONM, A_CORE = range(6)
B_XP, B_XM, B_ONP, B_ONM, B_Y, B_CORE = 0, 1, 2, 3, 4, 8
LATENT_COPIES = L_CORE + 6
A_COPIES = A_CORE + XS
B_COPIES = B_CORE + YS
GATHER_COPIES = max(A_COPIES, B_COPIES)
X_FIRST = (1, 3, 5)
TO_YH = ZS - 1
SUM_COPIES = ZS
LAST_COPIES = ZS * YHS - 1


def dot32(a, b):
    return jnp.dot(a, b, preferred_element_type=jnp.float32)


def dot32_nt(a, b):
    return lax.dot_general(a, b, NT, preferred_element_type=jnp.float32)


def layer_kernel(
    heads,
    tokens,
    pos_hbm,
    qn_hbm,
    qr_hbm,
    latent_hbm,
    rope_hbm,
    gain_hbm,
    uk_hbm,
    uv_hbm,
    wo_hbm,
    out_ref,
    pos_ref,
    latent_ref,
    rope_ref,
    gain_ref,
    qn_ref,
    qr_ref,
    uk_ref,
    uv_ref,
    wo_ref,
    kv,
    rope_t,
    pre,
    qa,
    qr,
    att,
    part,
    zbuf,
    mine,
    ysend,
    ybuf,
    last_part,
    lastbuf,
    result,
    load_sem,
    lsend,
    lrecv,
    gsend,
    grecv,
    rsend,
    rrecv,
    fsend,
    frecv,
    greeted,
):
    rows = qn_ref.shape[0]
    cols = out_ref.shape[0]
    rank = latent_ref.shape[1]
    keys = YS * XS * CORES * rows
    chunks = rows // tokens
    exponent = math.log2(math.e) / math.sqrt(NOPE + ROPE)

    ctx = lax.axis_index("ctx")
    head_group = lax.axis_index("head")
    y, x, core = ctx // (XS * CORES), (ctx // CORES) % XS, ctx % CORES
    z, yh = head_group // YHS, head_group % YHS
    x_next, x_last, x_far = (x + 1) % XS, (x + XS - 1) % XS, (x + 2) % XS

    def at_ctx(y_, x_, core_):
        return ((y_ * XS + x_) * CORES + core_, head_group)

    def at_head(z_, yh_):
        return (ctx, z_ * YHS + yh_)

    across = at_ctx(1 - y, x, core)
    ahead = at_ctx(y, x_next, core)
    behind = at_ctx(y, x_last, core)
    sibling = at_ctx(y, x, 1 - core)
    far = at_ctx(y, x_far, core)
    far_across = at_ctx(1 - y, x_far, core)
    across_over = (across[0], at_head(z, 1 - yh)[1])
    others = [(k // YHS, k % YHS) for k in range(1, ZS * YHS)]
    groups = [at_head((z + dz) % ZS, (yh + dy) % YHS) for dz, dy in others]
    over = groups[0]
    above = [groups[YHS * k - 1] for k in range(1, ZS)]

    barrier = pltpu.get_barrier_semaphore()
    partners = [across, ahead, behind, sibling, far, far_across, across_over, above[0], above[2]]
    for partner in partners:
        pl.semaphore_signal(barrier, inc=1, device_id=partner, device_id_type=MESH)

    loads = [
        pltpu.make_async_copy(source, target, load_sem.at[which])
        for which, (source, target) in enumerate(
            [
                (latent_hbm, latent_ref),
                (gain_hbm, gain_ref),
                (rope_hbm, rope_ref),
                (qn_hbm, qn_ref),
                (uk_hbm, uk_ref),
                (qr_hbm, qr_ref),
                (pos_hbm, pos_ref),
                (uv_hbm, uv_ref),
                (wo_hbm, wo_ref),
            ]
        )
    ]
    for load in loads:
        load.start()

    def remote(source, target, send, recv, partner):
        return pltpu.make_async_remote_copy(
            src_ref=source,
            dst_ref=target,
            send_sem=send,
            recv_sem=recv,
            device_id=partner,
            device_id_type=MESH,
        )

    def latent_copy(which):
        quarter = pl.ds(pl.multiple_of(z * (rank // ZS), rank // ZS), rank // ZS)
        lower, upper = pl.ds(0, rank // 2), pl.ds(rank // 2, rank // 2)
        if L_Z <= which < L_Z + ZS - 1:
            source = target = kv.at[pl.ds(6, 2), 0, :, quarter]
            partner = above[which - L_Z]
        else:
            source, target, partner = {
                L_FAR: (kv.at[0, 0, :, quarter], kv.at[6, 0, :, quarter], far),
                L_FAR_Y: (kv.at[0, 0, :, quarter], kv.at[7, 0, :, quarter], far_across),
                L_XP: (kv.at[0, 0], kv.at[2, 0], ahead),
                L_XM: (kv.at[0, 0], kv.at[3, 0], behind),
                L_Y1: (kv.at[0, 0, :, lower], kv.at[1, 0, :, lower], across),
                L_Y2: (kv.at[0, 0, :, upper], kv.at[1, 0, :, upper], across_over),
                L_YXP: (kv.at[1, 0], kv.at[4, 0], ahead),
                L_YXM: (kv.at[1, 0], kv.at[5, 0], behind),
                L_CORE: (kv.at[pl.ds(0, 2), 0], kv.at[pl.ds(0, 2), 1], sibling),
                L_CORE + 1: (kv.at[2, 0], kv.at[2, 1], sibling),
                L_CORE + 2: (kv.at[3, 0], kv.at[3, 1], sibling),
                L_CORE + 3: (kv.at[pl.ds(6, 2), 0], kv.at[pl.ds(6, 2), 1], sibling),
                L_CORE + 4: (kv.at[4, 0], kv.at[4, 1], sibling),
                L_CORE + 5: (kv.at[5, 0], kv.at[5, 1], sibling),
            }[which]
        return remote(source, target, lsend.at[which], lrecv.at[which], partner)

    def a_copy(index, which):
        slots = att.at[index]
        view, partner = {
            A_Y: (slots.at[y, x, core], across),
            A_XP: (slots.at[:, x, core], ahead),
            A_XM: (slots.at[:, x, core], behind),
            A_ONP: (slots.at[0, x_last, core], ahead),
            A_ONM: (slots.at[1, x_next, core], behind),
            A_CORE: (slots.at[:, x, core], sibling),
            A_CORE + 1: (slots.at[:, x_last, core], sibling),
            A_CORE + 2: (slots.at[:, x_next, core], sibling),
            A_CORE + 3: (slots.at[:, x_far, core], sibling),
        }[which]
        return remote(view, view, gsend.at[index, which], grecv.at[index, which], partner)

    def b_copy(index, which):
        slots = att.at[index]
        half = heads * VDIM // 2
        first, second = pl.ds(0, half), pl.ds(half, half)
        view, partner = {
            B_XP: (slots.at[y, x, core], ahead),
            B_XM: (slots.at[y, x, core], behind),
            B_ONP: (slots.at[y, x_last, core, :, first], ahead),
            B_ONM: (slots.at[y, x_next, core, :, second], behind),
            B_Y: (slots.at[y, x, core], across),
            B_Y + 1: (slots.at[y, x_last, core], across),
            B_Y + 2: (slots.at[y, x_next, core], across),
            B_Y + 3: (slots.at[y, x_far, core], across),
            B_CORE: (slots.at[y, :, core], sibling),
            B_CORE + 1: (slots.at[1 - y, :, core], sibling),
        }[which]
        return remote(view, view, gsend.at[index, which], grecv.at[index, which], partner)

    def sum_copy(index, which):
        send, recv = rsend.at[index, which], rrecv.at[index, which]
        if which == TO_YH:
            return remote(ysend.at[index], ybuf.at[index], send, recv, over)
        return remote(
            part.at[index, (z + which + 1) % ZS], zbuf.at[index, which], send, recv, above[which]
        )

    def last_copy(which):
        dz, dy = others[which]
        source = last_part.at[(z + dz) % ZS, (yh + dy) % YHS]
        return remote(source, lastbuf.at[which], fsend.at[which], frecv.at[which], groups[which])

    def start(copy, *copies):
        for which in copies:
            copy(which).start()

    def arrived(copy, *copies):
        for which in copies:
            copy(which).wait_recv()

    for load in loads[:3]:
        load.wait()
    latent = latent_ref[...].astype(jnp.float32)
    mean_square = jnp.mean(latent * latent, axis=1, keepdims=True)
    normed = (latent * lax.rsqrt(mean_square + 1e-06) * gain_ref[...]).astype(jnp.bfloat16)
    kv[0, 0, :rows] = normed
    parts = [rope_ref[k * PACKED : (k + 1) * PACKED] for k in range(ROPE // PACKED)]
    kv[0, 0, rows:] = jnp.concatenate(parts, axis=1)

    lane = lax.broadcasted_iota(jnp.int32, (rows, 2 * ROPE), 1)

    def project(head_list):
        for head in head_list:
            span = slice(head * NOPE, (head + 1) * NOPE)
            mixed = dot32_nt(qn_ref[:, span], uk_ref[:, span]).astype(jnp.bfloat16)
            qa[:, head] = mixed.reshape(chunks, tokens, rank)
            pair = qr_ref[:, (head // 2) * 2 * ROPE : (head // 2 + 1) * 2 * ROPE]
            rope = jnp.where(lane // ROPE == head % 2, pair, jnp.zeros_like(pair))
            qr[:, head] = rope.reshape(chunks, tokens, 2 * ROPE)

    for load in loads[3:7]:
        load.wait()
    project(range(heads // 2))
    pl.semaphore_wait(barrier, len(partners))
    start(latent_copy, L_FAR, L_FAR_Y, L_XP, L_XM, L_Y1, L_Y2)
    for neighbour in (above[0], above[2]):
        pl.semaphore_signal(greeted, inc=1, device_id=neighbour, device_id_type=MESH)
    project(range(heads // 2, heads))

    slots = YS * XS
    early = slots // 2 * CORES * rows
    key_ids = lax.broadcasted_iota(jnp.int32, (1, keys), 1)
    key_pos = key_ids % BLK
    for slot, (dy, dx) in enumerate(SLOTS):
        for side in range(CORES):
            owner = ((y + dy) % YS * XS + (x + dx) % XS) * CORES + (core + side) % CORES
            for k in range(rows // BLK):
                here = key_ids // BLK == (slot * CORES + side) * (rows // BLK) + k
                value = pos_ref[owner * (rows // BLK) + k] * BLK
                key_pos = jnp.where(here, key_pos + value, key_pos)

    def unpack_rope(slot_list):
        for slot in slot_list:
            for side in range(CORES):
                held = kv[slot, side, rows:]
                parts = [held[:, k * rows : (k + 1) * rows] for k in range(ROPE // PACKED)]
                first = (slot * CORES + side) * rows
                rope_t[:, first : first + rows] = jnp.concatenate(parts + parts, axis=0)

    def score(queries, rope, first_slot, last_slot):
        held = kv[first_slot:last_slot, :, :rows].reshape((last_slot - first_slot) * CORES * rows, rank)
        span = slice(first_slot * CORES * rows, last_slot * CORES * rows)
        return dot32_nt(queries, held) + dot32(rope, rope_t[:, span])

    def score_early(first_slot, last_slot):
        unpack_rope(range(first_slot, last_slot))
        span = slice(first_slot * CORES * rows, last_slot * CORES * rows)

        def pair(index, carry):
            two = pl.ds(2 * index, 2)
            value = score(
                qa[two].reshape(2 * heads * tokens, rank),
                qr[two].reshape(2 * heads * tokens, 2 * ROPE),
                first_slot,
                last_slot,
            )
            pre[two, :, span] = value.reshape(2, heads * tokens, value.shape[1])
            return carry

        lax.fori_loop(0, chunks // 2, pair, 0)

    arrived(latent_copy, L_Y1, L_Y2)
    start(latent_copy, L_YXP, L_YXM)
    arrived(latent_copy, L_FAR, L_FAR_Y)
    pl.semaphore_wait(greeted, 2)
    start(latent_copy, L_Z, L_Z + 1, L_Z + 2, L_CORE)
    for load in loads[7:]:
        load.wait()
    arrived(latent_copy, L_XP, L_XM)
    start(latent_copy, L_CORE + 1, L_CORE + 2)
    arrived(latent_copy, L_CORE)
    score_early(0, 2)
    arrived(latent_copy, L_CORE + 1, L_CORE + 2)
    score_early(2, 4)
    arrived(latent_copy, L_YXP, L_YXM)
    start(latent_copy, L_CORE + 4, L_CORE + 5)
    arrived(latent_copy, L_Z, L_Z + 1, L_Z + 2)
    start(latent_copy, L_CORE + 3)
    arrived(latent_copy, L_CORE + 4, L_CORE + 5)
    unpack_rope(range(4, 6))
    arrived(latent_copy, L_CORE + 3)
    unpack_rope(range(6, 8))

    def attend(index):
        first = index * tokens
        first_pos = pos_ref[ctx * (rows // BLK) + first // BLK] * BLK + first % BLK
        query_pos = first_pos + lax.broadcasted_iota(jnp.int32, (tokens, 1), 0)
        bias = jnp.where(key_pos <= query_pos, 0.0, FLOOR)
        queries = qa[index].reshape(heads * tokens, rank)
        late = score(queries, qr[index].reshape(heads * tokens, 2 * ROPE), slots // 2, slots)
        scores = jnp.concatenate([pre[index], late], axis=1)
        scores = scores.reshape(heads, tokens, keys) + bias[None]
        top = jnp.max(scores, axis=2, keepdims=True)
        weights = jnp.exp2((scores - top) * exponent)
        total = jnp.sum(weights, axis=2, keepdims=True)
        weights = weights.astype(jnp.bfloat16).reshape(heads * tokens, keys)
        mixed = dot32(weights, kv[:, :, :rows].reshape(keys, rank))
        mixed = (mixed.reshape(heads, tokens, rank) / total).astype(jnp.bfloat16)
        for head in range(heads):
            span = slice(head * VDIM, (head + 1) * VDIM)
            att[index, y, x, core, :, span] = dot32(mixed[head], uv_ref[:, span]).astype(
                jnp.bfloat16
            )

    def a_own(index, copy):
        start(copy, A_Y)

    def a_across(index, copy):
        arrived(copy, A_Y)
        start(copy, A_XP, A_XM, A_CORE)

    def a_along(index, copy):
        arrived(copy, A_XP, A_XM)
        start(copy, A_ONP, A_ONM, A_CORE + 1, A_CORE + 2)

    def a_onward(index, copy):
        arrived(copy, A_ONP, A_ONM)
        start(copy, A_CORE + 3)

    def a_all(index, copy):
        arrived(copy, *range(A_CORE, A_CORE + XS))

    def b_own(index, copy):
        start(copy, B_XP, B_XM, B_Y)

    def b_along(index, copy):
        arrived(copy, B_XP, B_XM)
        start(copy, B_ONP, B_ONM, B_Y + 1, B_Y + 2)

    def b_onward(index, copy):
        arrived(copy, B_ONP, B_ONM)
        start(copy, B_Y + 3, B_CORE)

    def b_across(index, copy):
        arrived(copy, *range(B_Y, B_Y + XS))
        start(copy, B_CORE + 1)

    def b_all(index, copy):
        arrived(copy, *range(B_CORE, B_CORE + YS))

    def multiply(index, copy):
        held = att[index].reshape(YS * XS * CORES * tokens, heads * VDIM)
        product = dot32_nt(held, wo_ref[...]).astype(jnp.bfloat16)
        product = product.reshape(ZS, YHS, CORES * tokens, cols)
        if isinstance(index, int) and index == chunks - 1:
            last_part[...] = product
            start(last_copy, *range(LAST_COPIES))
        else:
            part[index] = jnp.concatenate([product[:, 0], product[:, 1]], axis=2)
            start(functools.partial(sum_copy, index), *range(ZS - 1))

    def sum_z(index, copy):
        for which in range(ZS - 1):
            sum_copy(index, which).wait_recv()

        value = part[index, z].astype(jnp.float32)
        for which in range(ZS - 1):
            value += zbuf[index, which].astype(jnp.float32)
        lower, upper = value[:, :cols], value[:, cols:]
        ysend[index] = jnp.where(yh == 0, upper, lower).astype(jnp.bfloat16)
        sum_copy(index, TO_YH).start()
        mine[index] = jnp.where(yh == 0, lower, upper)

    def finish(index, copy):
        sum_copy(index, TO_YH).wait_recv()
        value = mine[index] + ybuf[index].astype(jnp.float32)
        place_rows(index, value)

    def place_rows(index, value):
        for which in range(CORES):
            place = pl.ds(pl.multiple_of(which * rows + index * tokens, tokens), tokens)
            result[place, :cols] = value[which * tokens : (which + 1) * tokens]

    def finish_last():
        arrived(last_copy, *range(LAST_COPIES))
        value = last_part[z, yh].astype(jnp.float32)
        for which in range(LAST_COPIES):
            value += lastbuf[which].astype(jnp.float32)
        place_rows(chunks - 1, value)

    def gather_sent():
        for which in range(LATENT_COPIES):
            latent_copy(which).wait_send()
        for index in range(chunks):
            copy = functools.partial(b_copy if index in X_FIRST else a_copy, index)
            for which in range(B_COPIES if index in X_FIRST else A_COPIES):
                copy(which).wait_send()

    def step(turn, carry):
        def stage(body, taken):
            index = -1
            for round_, chunk in enumerate(taken):
                if chunk >= 0:
                    index = jnp.where(turn == round_, chunk, index)

            @pl.when(index >= 0)
            def _():
                copy = b_copy if body.__name__.startswith("b_") else a_copy
                body(index, functools.partial(copy, index))

        attend(turn)
        stage(a_own, [-1 if k in X_FIRST else k for k in range(chunks)])
        stage(b_own, [k if k in X_FIRST else -1 for k in range(chunks)])
        stage(a_onward, [-1, -1, -1, -1, -1, -1, -1, 0])
        stage(a_along, [-1, -1, -1, -1, -1, 0, -1, 2])
        stage(b_across, [-1, -1, -1, -1, -1, -1, -1, 1])
        stage(a_across, [-1, -1, 0, -1, 2, -1, 4, -1])
        stage(b_onward, [-1, -1, -1, -1, -1, 1, -1, 3])
        stage(b_along, [-1, -1, -1, 1, -1, 3, -1, 5])
        return carry

    lax.fori_loop(0, chunks, step, 0)

    rest = [
        (a_all, 0),
        (multiply, 0),
        (a_along, 4),
        (b_all, 1),
        (multiply, 1),
        (a_across, 6),
        (a_onward, 2),
        (b_onward, 5),
        (a_across, 7),
        (a_all, 2),
        (multiply, 2),
        (a_onward, 4),
        (b_across, 3),
        (sum_z, 0),
        (a_all, 4),
        (multiply, 4),
        (sum_z, 1),
        (a_along, 6),
        (b_all, 3),
        (multiply, 3),
        (b_across, 5),
        (sum_z, 2),
        (finish, 0),
        (a_along, 7),
        (finish, 1),
        (b_all, 5),
        (multiply, 5),
        (a_onward, 6),
        (sum_z, 4),
        (finish, 2),
        (a_onward, 7),
        (a_all, 6),
        (multiply, 6),
        (sum_z, 3),
        (finish, 4),
        (a_all, 7),
        (multiply, 7),
        (sum_z, 5),
        (finish, 3),
        (sum_z, 6),
        (finish, 5),
        (finish, 6),
    ]
    for body, index in rest:
        body(index, functools.partial(b_copy if index in X_FIRST else a_copy, index))
        if body is multiply and index == chunks - 1:
            gather_sent()
    for index in range(chunks - 1):
        for which in range(SUM_COPIES):
            sum_copy(index, which).wait_send()
    finish_last()
    out_ref[...] = result[...].T[:cols].astype(jnp.bfloat16)
    for which in range(LAST_COPIES):
        last_copy(which).wait_send()


TOKENS = 16


def shards(q_nope, q_rope, latent, k_rope, kv_gain, w_uk, w_uv, w_out, block_pos):
    rows = q_nope.shape[0]
    heads = w_uk.shape[1] // NOPE
    rank = latent.shape[1]
    cols = w_out.shape[1]
    chunks = rows // TOKENS
    vmem = pl.BlockSpec(memory_space=pltpu.VMEM)
    hbm = pl.BlockSpec(memory_space=pl.ANY)
    return pl.pallas_call(
        functools.partial(layer_kernel, heads, TOKENS),
        name="layer",
        out_shape=jax.ShapeDtypeStruct((cols, CORES * rows), jnp.bfloat16),
        in_specs=[hbm] * 9,
        out_specs=vmem,
        scratch_shapes=[
            pltpu.SMEM(block_pos.shape, block_pos.dtype),
            pltpu.VMEM(latent.shape, latent.dtype),
            pltpu.VMEM(k_rope.shape[::-1], k_rope.dtype),
            pltpu.VMEM((1, rank), kv_gain.dtype),
            pltpu.VMEM(q_nope.shape, q_nope.dtype),
            pltpu.VMEM(q_rope.shape, q_rope.dtype),
            pltpu.VMEM(w_uk.shape, w_uk.dtype),
            pltpu.VMEM(w_uv.shape, w_uv.dtype),
            pltpu.VMEM((cols, heads * VDIM), w_out.dtype),
            pltpu.VMEM((YS * XS, CORES, rows + PACKED, rank), jnp.bfloat16),
            pltpu.VMEM((2 * ROPE, YS * XS * CORES * rows), jnp.bfloat16),
            pltpu.VMEM((chunks, heads * TOKENS, YS * XS * CORES * rows // 2), jnp.float32),
            pltpu.VMEM((chunks, heads, TOKENS, rank), jnp.bfloat16),
            pltpu.VMEM((chunks, heads, TOKENS, 2 * ROPE), jnp.bfloat16),
            pltpu.VMEM((chunks, YS, XS, CORES, TOKENS, heads * VDIM), jnp.bfloat16),
            pltpu.VMEM((chunks, ZS, CORES * TOKENS, YHS * cols), jnp.bfloat16),
            pltpu.VMEM((chunks, ZS - 1, CORES * TOKENS, YHS * cols), jnp.bfloat16),
            pltpu.VMEM((chunks, CORES * TOKENS, cols), jnp.float32),
            pltpu.VMEM((chunks, CORES * TOKENS, cols), jnp.bfloat16),
            pltpu.VMEM((chunks, CORES * TOKENS, cols), jnp.bfloat16),
            pltpu.VMEM((ZS, YHS, CORES * TOKENS, cols), jnp.bfloat16),
            pltpu.VMEM((LAST_COPIES, CORES * TOKENS, cols), jnp.bfloat16),
            pltpu.VMEM((CORES * rows, pl.cdiv(cols, 128) * 128), jnp.float32),
            pltpu.SemaphoreType.DMA((9,)),
            pltpu.SemaphoreType.DMA((LATENT_COPIES,)),
            pltpu.SemaphoreType.DMA((LATENT_COPIES,)),
            pltpu.SemaphoreType.DMA((chunks, GATHER_COPIES)),
            pltpu.SemaphoreType.DMA((chunks, GATHER_COPIES)),
            pltpu.SemaphoreType.DMA((chunks, SUM_COPIES)),
            pltpu.SemaphoreType.DMA((chunks, SUM_COPIES)),
            pltpu.SemaphoreType.DMA((LAST_COPIES,)),
            pltpu.SemaphoreType.DMA((LAST_COPIES,)),
            pltpu.SemaphoreType.REGULAR,
        ],
        compiler_params=pltpu.CompilerParams(
            collective_id=0, has_side_effects=True, vmem_limit_bytes=60 * 2**20
        ),
    )(block_pos, q_nope, q_rope, latent, k_rope.T, kv_gain[None, :], w_uk, w_uv, w_out.T).T


def solution(mesh):
    placed = (
        P("ctx", "head"),
        P("ctx", "head"),
        P("ctx", None),
        P("ctx", None),
        P(),
        P(None, "head"),
        P(None, "head"),
        P("head", "ctx"),
        P(),
    )
    return jax.shard_map(
        shards, mesh=mesh, in_specs=placed, out_specs=P("head", "ctx"), check_vma=False
    )
```

```python
import functools
import math

import jax
import jax.numpy as jnp
from jax import lax
from jax.experimental import pallas as pl
from jax.experimental.pallas import tpu as pltpu
from jax.sharding import PartitionSpec as P

NOPE = 128
ROPE = 64
VDIM = 128
BLK = 64
FLOOR = -1e30
NT = (((1,), (1,)), ((), ()))
MESH = pl.DeviceIdType.MESH

YS, XS, CORES, ZS, YHS = 2, 4, 2, 4, 2
SLOTS = ((0, 0), (1, 0), (0, 3), (0, 1), (1, 3), (1, 1), (0, 2), (1, 2))
PACKED = 16
L_FAR, L_FAR_Y, L_XP, L_XM, L_Y1, L_Y2, L_YXP, L_YXM, L_Z, L_CORE = 0, 1, 2, 3, 4, 5, 6, 7, 8, 11
A_Y, A_XP, A_XM, A_ONP, A_ONM, A_CORE = range(6)
B_XP, B_XM, B_ONP, B_ONM, B_Y, B_CORE = 0, 1, 2, 3, 4, 8
LATENT_COPIES = L_CORE + 6
A_COPIES = A_CORE + XS
B_COPIES = B_CORE + YS
GATHER_COPIES = max(A_COPIES, B_COPIES)
X_FIRST = (1, 3, 5)
TO_YH = ZS - 1
SUM_COPIES = ZS
LAST_COPIES = ZS * YHS - 1


def dot32(a, b):
    return jnp.dot(a, b, preferred_element_type=jnp.float32)


def dot32_nt(a, b):
    return lax.dot_general(a, b, NT, preferred_element_type=jnp.float32)


def layer_kernel(
    heads,
    tokens,
    pos_hbm,
    qn_hbm,
    qr_hbm,
    latent_hbm,
    rope_hbm,
    gain_hbm,
    uk_hbm,
    uv_hbm,
    wo_hbm,
    out_ref,
    pos_ref,
    latent_ref,
    rope_ref,
    gain_ref,
    qn_ref,
    qr_ref,
    uk_ref,
    uv_ref,
    wo_ref,
    kv,
    rope_t,
    pre,
    qa,
    qr,
    att,
    part,
    zbuf,
    mine,
    ysend,
    ybuf,
    last_part,
    lastbuf,
    result,
    load_sem,
    lsend,
    lrecv,
    gsend,
    grecv,
    rsend,
    rrecv,
    fsend,
    frecv,
    greeted,
):
    rows = qn_ref.shape[0]
    cols = out_ref.shape[0]
    rank = latent_ref.shape[1]
    keys = YS * XS * CORES * rows
    chunks = rows // tokens
    exponent = math.log2(math.e) / math.sqrt(NOPE + ROPE)

    ctx = lax.axis_index("ctx")
    head_group = lax.axis_index("head")
    y, x, core = ctx // (XS * CORES), (ctx // CORES) % XS, ctx % CORES
    z, yh = head_group // YHS, head_group % YHS
    x_next, x_last, x_far = (x + 1) % XS, (x + XS - 1) % XS, (x + 2) % XS

    def at_ctx(y_, x_, core_):
        return ((y_ * XS + x_) * CORES + core_, head_group)

    def at_head(z_, yh_):
        return (ctx, z_ * YHS + yh_)

    across = at_ctx(1 - y, x, core)
    ahead = at_ctx(y, x_next, core)
    behind = at_ctx(y, x_last, core)
    sibling = at_ctx(y, x, 1 - core)
    far = at_ctx(y, x_far, core)
    far_across = at_ctx(1 - y, x_far, core)
    across_over = (across[0], at_head(z, 1 - yh)[1])
    others = [(k // YHS, k % YHS) for k in range(1, ZS * YHS)]
    groups = [at_head((z + dz) % ZS, (yh + dy) % YHS) for dz, dy in others]
    over = groups[0]
    above = [groups[YHS * k - 1] for k in range(1, ZS)]

    barrier = pltpu.get_barrier_semaphore()
    partners = [across, ahead, behind, sibling, far, far_across, across_over, above[0], above[2]]
    for partner in partners:
        pl.semaphore_signal(barrier, inc=1, device_id=partner, device_id_type=MESH)

    loads = [
        pltpu.make_async_copy(source, target, load_sem.at[which])
        for which, (source, target) in enumerate(
            [
                (latent_hbm, latent_ref),
                (gain_hbm, gain_ref),
                (rope_hbm, rope_ref),
                (qn_hbm, qn_ref),
                (uk_hbm, uk_ref),
                (qr_hbm, qr_ref),
                (pos_hbm, pos_ref),
                (uv_hbm, uv_ref),
                (wo_hbm, wo_ref),
            ]
        )
    ]
    for load in loads:
        load.start()

    def remote(source, target, send, recv, partner):
        return pltpu.make_async_remote_copy(
            src_ref=source,
            dst_ref=target,
            send_sem=send,
            recv_sem=recv,
            device_id=partner,
            device_id_type=MESH,
        )

    def latent_copy(which):
        quarter = pl.ds(pl.multiple_of(z * (rank // ZS), rank // ZS), rank // ZS)
        lower, upper = pl.ds(0, rank // 2), pl.ds(rank // 2, rank // 2)
        if L_Z <= which < L_Z + ZS - 1:
            source = target = kv.at[pl.ds(6, 2), 0, :, quarter]
            partner = above[which - L_Z]
        else:
            source, target, partner = {
                L_FAR: (kv.at[0, 0, :, quarter], kv.at[6, 0, :, quarter], far),
                L_FAR_Y: (kv.at[0, 0, :, quarter], kv.at[7, 0, :, quarter], far_across),
                L_XP: (kv.at[0, 0], kv.at[2, 0], ahead),
                L_XM: (kv.at[0, 0], kv.at[3, 0], behind),
                L_Y1: (kv.at[0, 0, :, lower], kv.at[1, 0, :, lower], across),
                L_Y2: (kv.at[0, 0, :, upper], kv.at[1, 0, :, upper], across_over),
                L_YXP: (kv.at[1, 0], kv.at[4, 0], ahead),
                L_YXM: (kv.at[1, 0], kv.at[5, 0], behind),
                L_CORE: (kv.at[pl.ds(0, 2), 0], kv.at[pl.ds(0, 2), 1], sibling),
                L_CORE + 1: (kv.at[2, 0], kv.at[2, 1], sibling),
                L_CORE + 2: (kv.at[3, 0], kv.at[3, 1], sibling),
                L_CORE + 3: (kv.at[pl.ds(6, 2), 0], kv.at[pl.ds(6, 2), 1], sibling),
                L_CORE + 4: (kv.at[4, 0], kv.at[4, 1], sibling),
                L_CORE + 5: (kv.at[5, 0], kv.at[5, 1], sibling),
            }[which]
        return remote(source, target, lsend.at[which], lrecv.at[which], partner)

    def a_copy(index, which):
        slots = att.at[index]
        view, partner = {
            A_Y: (slots.at[y, x, core], across),
            A_XP: (slots.at[:, x, core], ahead),
            A_XM: (slots.at[:, x, core], behind),
            A_ONP: (slots.at[0, x_last, core], ahead),
            A_ONM: (slots.at[1, x_next, core], behind),
            A_CORE: (slots.at[:, x, core], sibling),
            A_CORE + 1: (slots.at[:, x_last, core], sibling),
            A_CORE + 2: (slots.at[:, x_next, core], sibling),
            A_CORE + 3: (slots.at[:, x_far, core], sibling),
        }[which]
        return remote(view, view, gsend.at[index, which], grecv.at[index, which], partner)

    def b_copy(index, which):
        slots = att.at[index]
        half = heads * VDIM // 2
        first, second = pl.ds(0, half), pl.ds(half, half)
        view, partner = {
            B_XP: (slots.at[y, x, core], ahead),
            B_XM: (slots.at[y, x, core], behind),
            B_ONP: (slots.at[y, x_last, core, :, first], ahead),
            B_ONM: (slots.at[y, x_next, core, :, second], behind),
            B_Y: (slots.at[y, x, core], across),
            B_Y + 1: (slots.at[y, x_last, core], across),
            B_Y + 2: (slots.at[y, x_next, core], across),
            B_Y + 3: (slots.at[y, x_far, core], across),
            B_CORE: (slots.at[y, :, core], sibling),
            B_CORE + 1: (slots.at[1 - y, :, core], sibling),
        }[which]
        return remote(view, view, gsend.at[index, which], grecv.at[index, which], partner)

    def sum_copy(index, which):
        send, recv = rsend.at[index, which], rrecv.at[index, which]
        if which == TO_YH:
            return remote(ysend.at[index], ybuf.at[index], send, recv, over)
        return remote(
            part.at[index, (z + which + 1) % ZS], zbuf.at[index, which], send, recv, above[which]
        )

    def last_copy(which):
        dz, dy = others[which]
        source = last_part.at[(z + dz) % ZS, (yh + dy) % YHS]
        return remote(source, lastbuf.at[which], fsend.at[which], frecv.at[which], groups[which])

    def start(copy, *copies):
        for which in copies:
            copy(which).start()

    def arrived(copy, *copies):
        for which in copies:
            copy(which).wait_recv()

    for load in loads[:3]:
        load.wait()
    latent = latent_ref[...].astype(jnp.float32)
    mean_square = jnp.mean(latent * latent, axis=1, keepdims=True)
    normed = (latent * lax.rsqrt(mean_square + 1e-06) * gain_ref[...]).astype(jnp.bfloat16)
    kv[0, 0, :rows] = normed
    parts = [rope_ref[k * PACKED : (k + 1) * PACKED] for k in range(ROPE // PACKED)]
    kv[0, 0, rows:] = jnp.concatenate(parts, axis=1)

    lane = lax.broadcasted_iota(jnp.int32, (rows, 2 * ROPE), 1)

    def project(head_list):
        for head in head_list:
            span = slice(head * NOPE, (head + 1) * NOPE)
            mixed = dot32_nt(qn_ref[:, span], uk_ref[:, span]).astype(jnp.bfloat16)
            qa[:, head] = mixed.reshape(chunks, tokens, rank)
            pair = qr_ref[:, (head // 2) * 2 * ROPE : (head // 2 + 1) * 2 * ROPE]
            rope = jnp.where(lane // ROPE == head % 2, pair, jnp.zeros_like(pair))
            qr[:, head] = rope.reshape(chunks, tokens, 2 * ROPE)

    for load in loads[3:7]:
        load.wait()
    project(range(heads // 2))
    pl.semaphore_wait(barrier, len(partners))
    start(latent_copy, L_FAR, L_FAR_Y, L_XP, L_XM, L_Y1, L_Y2)
    for neighbour in (above[0], above[2]):
        pl.semaphore_signal(greeted, inc=1, device_id=neighbour, device_id_type=MESH)
    project(range(heads // 2, heads))

    slots = YS * XS
    early = slots // 2 * CORES * rows
    key_ids = lax.broadcasted_iota(jnp.int32, (1, keys), 1)
    key_pos = key_ids % BLK
    for slot, (dy, dx) in enumerate(SLOTS):
        for side in range(CORES):
            owner = ((y + dy) % YS * XS + (x + dx) % XS) * CORES + (core + side) % CORES
            for k in range(rows // BLK):
                here = key_ids // BLK == (slot * CORES + side) * (rows // BLK) + k
                value = pos_ref[owner * (rows // BLK) + k] * BLK
                key_pos = jnp.where(here, key_pos + value, key_pos)

    def unpack_rope(slot_list):
        for slot in slot_list:
            for side in range(CORES):
                held = kv[slot, side, rows:]
                parts = [held[:, k * rows : (k + 1) * rows] for k in range(ROPE // PACKED)]
                first = (slot * CORES + side) * rows
                rope_t[:, first : first + rows] = jnp.concatenate(parts + parts, axis=0)

    def score(queries, rope, first_slot, last_slot):
        held = kv[first_slot:last_slot, :, :rows].reshape((last_slot - first_slot) * CORES * rows, rank)
        span = slice(first_slot * CORES * rows, last_slot * CORES * rows)
        return dot32_nt(queries, held) + dot32(rope, rope_t[:, span])

    def score_early(first_slot, last_slot):
        unpack_rope(range(first_slot, last_slot))
        span = slice(first_slot * CORES * rows, last_slot * CORES * rows)

        def pair(index, carry):
            two = pl.ds(2 * index, 2)
            value = score(
                qa[two].reshape(2 * heads * tokens, rank),
                qr[two].reshape(2 * heads * tokens, 2 * ROPE),
                first_slot,
                last_slot,
            )
            pre[two, :, span] = value.reshape(2, heads * tokens, value.shape[1])
            return carry

        lax.fori_loop(0, chunks // 2, pair, 0)

    arrived(latent_copy, L_Y1, L_Y2)
    start(latent_copy, L_YXP, L_YXM)
    arrived(latent_copy, L_FAR, L_FAR_Y)
    pl.semaphore_wait(greeted, 2)
    start(latent_copy, L_Z, L_Z + 1, L_Z + 2, L_CORE)
    for load in loads[7:]:
        load.wait()
    arrived(latent_copy, L_XP, L_XM)
    start(latent_copy, L_CORE + 1, L_CORE + 2)
    arrived(latent_copy, L_CORE)
    score_early(0, 2)
    arrived(latent_copy, L_CORE + 1, L_CORE + 2)
    score_early(2, 4)
    arrived(latent_copy, L_YXP, L_YXM)
    start(latent_copy, L_CORE + 4, L_CORE + 5)
    arrived(latent_copy, L_Z, L_Z + 1, L_Z + 2)
    start(latent_copy, L_CORE + 3)
    arrived(latent_copy, L_CORE + 4, L_CORE + 5)
    unpack_rope(range(4, 6))
    arrived(latent_copy, L_CORE + 3)
    unpack_rope(range(6, 8))

    def attend(index):
        first = index * tokens
        first_pos = pos_ref[ctx * (rows // BLK) + first // BLK] * BLK + first % BLK
        query_pos = first_pos + lax.broadcasted_iota(jnp.int32, (tokens, 1), 0)
        bias = jnp.where(key_pos <= query_pos, 0.0, FLOOR)
        queries = qa[index].reshape(heads * tokens, rank)
        late = score(queries, qr[index].reshape(heads * tokens, 2 * ROPE), slots // 2, slots)
        scores = jnp.concatenate([pre[index], late], axis=1)
        scores = scores.reshape(heads, tokens, keys) + bias[None]
        top = jnp.max(scores, axis=2, keepdims=True)
        weights = jnp.exp2((scores - top) * exponent)
        total = jnp.sum(weights, axis=2, keepdims=True)
        weights = weights.astype(jnp.bfloat16).reshape(heads * tokens, keys)
        mixed = dot32(weights, kv[:, :, :rows].reshape(keys, rank))
        mixed = (mixed.reshape(heads, tokens, rank) / total).astype(jnp.bfloat16)
        for head in range(heads):
            span = slice(head * VDIM, (head + 1) * VDIM)
            att[index, y, x, core, :, span] = dot32(mixed[head], uv_ref[:, span]).astype(
                jnp.bfloat16
            )

    def a_own(index, copy):
        start(copy, A_Y)

    def a_across(index, copy):
        arrived(copy, A_Y)
        start(copy, A_XP, A_XM, A_CORE)

    def a_along(index, copy):
        arrived(copy, A_XP, A_XM)
        start(copy, A_ONP, A_ONM, A_CORE + 1, A_CORE + 2)

    def a_onward(index, copy):
        arrived(copy, A_ONP, A_ONM)
        start(copy, A_CORE + 3)

    def a_all(index, copy):
        arrived(copy, *range(A_CORE, A_CORE + XS))

    def b_own(index, copy):
        start(copy, B_XP, B_XM, B_Y)

    def b_along(index, copy):
        arrived(copy, B_XP, B_XM)
        start(copy, B_ONP, B_ONM, B_Y + 1, B_Y + 2)

    def b_onward(index, copy):
        arrived(copy, B_ONP, B_ONM)
        start(copy, B_Y + 3, B_CORE)

    def b_across(index, copy):
        arrived(copy, *range(B_Y, B_Y + XS))
        start(copy, B_CORE + 1)

    def b_all(index, copy):
        arrived(copy, *range(B_CORE, B_CORE + YS))

    def multiply(index, copy):
        held = att[index].reshape(YS * XS * CORES * tokens, heads * VDIM)
        product = dot32_nt(held, wo_ref[...]).astype(jnp.bfloat16)
        product = product.reshape(ZS, YHS, CORES * tokens, cols)
        if isinstance(index, int) and index == chunks - 1:
            last_part[...] = product
            start(last_copy, *range(LAST_COPIES))
        else:
            part[index] = jnp.concatenate([product[:, 0], product[:, 1]], axis=2)
            start(functools.partial(sum_copy, index), 2, 1, 0)

    def sum_z(index, copy):
        for which in range(ZS - 1):
            sum_copy(index, which).wait_recv()

        value = part[index, z].astype(jnp.float32)
        for which in range(ZS - 1):
            value += zbuf[index, which].astype(jnp.float32)
        lower, upper = value[:, :cols], value[:, cols:]
        ysend[index] = jnp.where(yh == 0, upper, lower).astype(jnp.bfloat16)
        sum_copy(index, TO_YH).start()
        mine[index] = jnp.where(yh == 0, lower, upper)

    def finish(index, copy):
        sum_copy(index, TO_YH).wait_recv()
        value = mine[index] + ybuf[index].astype(jnp.float32)
        place_rows(index, value)

    def place_rows(index, value):
        for which in range(CORES):
            place = pl.ds(pl.multiple_of(which * rows + index * tokens, tokens), tokens)
            result[place, :cols] = value[which * tokens : (which + 1) * tokens]

    def finish_last():
        arrived(last_copy, *range(LAST_COPIES))
        value = last_part[z, yh].astype(jnp.float32)
        for which in range(LAST_COPIES):
            value += lastbuf[which].astype(jnp.float32)
        place_rows(chunks - 1, value)

    def gather_sent():
        for which in range(LATENT_COPIES):
            latent_copy(which).wait_send()
        for index in range(chunks):
            copy = functools.partial(b_copy if index in X_FIRST else a_copy, index)
            for which in range(B_COPIES if index in X_FIRST else A_COPIES):
                copy(which).wait_send()

    def step(turn, carry):
        def stage(body, taken):
            index = -1
            for round_, chunk in enumerate(taken):
                if chunk >= 0:
                    index = jnp.where(turn == round_, chunk, index)

            @pl.when(index >= 0)
            def _():
                copy = b_copy if body.__name__.startswith("b_") else a_copy
                body(index, functools.partial(copy, index))

        attend(turn)
        stage(a_own, [-1 if k in X_FIRST else k for k in range(chunks)])
        stage(b_own, [k if k in X_FIRST else -1 for k in range(chunks)])
        stage(a_onward, [-1, -1, -1, -1, -1, -1, -1, 0])
        stage(b_onward, [-1, -1, -1, -1, -1, 1, -1, 3])
        stage(a_across, [-1, -1, 0, -1, 2, -1, 4, -1])
        stage(b_along, [-1, -1, -1, 1, -1, 3, -1, 5])
        stage(a_along, [-1, -1, -1, -1, 0, -1, 2, -1])
        return carry

    lax.fori_loop(0, chunks, step, 0)

    rest = [
        (b_across, 1),
        (a_all, 0),
        (multiply, 0),
        (a_along, 4),
        (b_all, 1),
        (multiply, 1),
        (a_across, 6),
        (a_onward, 2),
        (b_onward, 5),
        (a_across, 7),
        (a_all, 2),
        (multiply, 2),
        (a_onward, 4),
        (b_across, 3),
        (sum_z, 0),
        (a_all, 4),
        (multiply, 4),
        (sum_z, 1),
        (a_along, 6),
        (b_all, 3),
        (multiply, 3),
        (b_across, 5),
        (sum_z, 2),
        (finish, 0),
        (a_along, 7),
        (finish, 1),
        (b_all, 5),
        (multiply, 5),
        (a_onward, 6),
        (sum_z, 4),
        (finish, 2),
        (a_onward, 7),
        (a_all, 6),
        (multiply, 6),
        (sum_z, 3),
        (finish, 4),
        (a_all, 7),
        (multiply, 7),
        (sum_z, 5),
        (finish, 3),
        (sum_z, 6),
        (finish, 5),
        (finish, 6),
    ]
    for body, index in rest:
        body(index, functools.partial(b_copy if index in X_FIRST else a_copy, index))
        if body is multiply and index == chunks - 1:
            gather_sent()
    for index in range(chunks - 1):
        for which in range(SUM_COPIES):
            sum_copy(index, which).wait_send()
    finish_last()
    out_ref[...] = result[...].T[:cols].astype(jnp.bfloat16)
    for which in range(LAST_COPIES):
        last_copy(which).wait_send()


TOKENS = 16


def shards(q_nope, q_rope, latent, k_rope, kv_gain, w_uk, w_uv, w_out, block_pos):
    rows = q_nope.shape[0]
    heads = w_uk.shape[1] // NOPE
    rank = latent.shape[1]
    cols = w_out.shape[1]
    chunks = rows // TOKENS
    vmem = pl.BlockSpec(memory_space=pltpu.VMEM)
    hbm = pl.BlockSpec(memory_space=pl.ANY)
    return pl.pallas_call(
        functools.partial(layer_kernel, heads, TOKENS),
        name="layer",
        out_shape=jax.ShapeDtypeStruct((cols, CORES * rows), jnp.bfloat16),
        in_specs=[hbm] * 9,
        out_specs=vmem,
        scratch_shapes=[
            pltpu.SMEM(block_pos.shape, block_pos.dtype),
            pltpu.VMEM(latent.shape, latent.dtype),
            pltpu.VMEM(k_rope.shape[::-1], k_rope.dtype),
            pltpu.VMEM((1, rank), kv_gain.dtype),
            pltpu.VMEM(q_nope.shape, q_nope.dtype),
            pltpu.VMEM(q_rope.shape, q_rope.dtype),
            pltpu.VMEM(w_uk.shape, w_uk.dtype),
            pltpu.VMEM(w_uv.shape, w_uv.dtype),
            pltpu.VMEM((cols, heads * VDIM), w_out.dtype),
            pltpu.VMEM((YS * XS, CORES, rows + PACKED, rank), jnp.bfloat16),
            pltpu.VMEM((2 * ROPE, YS * XS * CORES * rows), jnp.bfloat16),
            pltpu.VMEM((chunks, heads * TOKENS, YS * XS * CORES * rows // 2), jnp.float32),
            pltpu.VMEM((chunks, heads, TOKENS, rank), jnp.bfloat16),
            pltpu.VMEM((chunks, heads, TOKENS, 2 * ROPE), jnp.bfloat16),
            pltpu.VMEM((chunks, YS, XS, CORES, TOKENS, heads * VDIM), jnp.bfloat16),
            pltpu.VMEM((chunks, ZS, CORES * TOKENS, YHS * cols), jnp.bfloat16),
            pltpu.VMEM((chunks, ZS - 1, CORES * TOKENS, YHS * cols), jnp.bfloat16),
            pltpu.VMEM((chunks, CORES * TOKENS, cols), jnp.float32),
            pltpu.VMEM((chunks, CORES * TOKENS, cols), jnp.bfloat16),
            pltpu.VMEM((chunks, CORES * TOKENS, cols), jnp.bfloat16),
            pltpu.VMEM((ZS, YHS, CORES * TOKENS, cols), jnp.bfloat16),
            pltpu.VMEM((LAST_COPIES, CORES * TOKENS, cols), jnp.bfloat16),
            pltpu.VMEM((CORES * rows, pl.cdiv(cols, 128) * 128), jnp.float32),
            pltpu.SemaphoreType.DMA((9,)),
            pltpu.SemaphoreType.DMA((LATENT_COPIES,)),
            pltpu.SemaphoreType.DMA((LATENT_COPIES,)),
            pltpu.SemaphoreType.DMA((chunks, GATHER_COPIES)),
            pltpu.SemaphoreType.DMA((chunks, GATHER_COPIES)),
            pltpu.SemaphoreType.DMA((chunks, SUM_COPIES)),
            pltpu.SemaphoreType.DMA((chunks, SUM_COPIES)),
            pltpu.SemaphoreType.DMA((LAST_COPIES,)),
            pltpu.SemaphoreType.DMA((LAST_COPIES,)),
            pltpu.SemaphoreType.REGULAR,
        ],
        compiler_params=pltpu.CompilerParams(
            collective_id=0, has_side_effects=True, vmem_limit_bytes=60 * 2**20
        ),
    )(block_pos, q_nope, q_rope, latent, k_rope.T, kv_gain[None, :], w_uk, w_uv, w_out.T).T


def solution(mesh):
    placed = (
        P("ctx", "head"),
        P("ctx", "head"),
        P("ctx", None),
        P("ctx", None),
        P(),
        P(None, "head"),
        P(None, "head"),
        P("head", "ctx"),
        P(),
    )
    return jax.shard_map(
        shards, mesh=mesh, in_specs=placed, out_specs=P("head", "ctx"), check_vma=False
    )
```
